128 devices in a mesh: visit: 4 (over x), patch: 32 (over z, y, core).
Axes of the slice: x: 4, y: 4, z: 4, core: 2. Of those that a mesh axis runs over, the one named last changes fastest.
Arguments:
- warp_image: float32 [3072, 84, 512], P(('visit', 'patch')), may hold values from -6 to 6
- warp_variance: float32 [3072, 64, 512], P(('visit', 'patch')), may hold values from 0.25 to 4
- kernel_coef: float32 [3072, 40], P(('visit', 'patch')), may hold values from -0.6 to 0.6
- tile_patch: int32 [3072, 1], P(('visit', 'patch')), may hold values from 0 to 31; in each aligned block of 24 rows (0 to 23, 24 to 47, ...) at most 2 rows name the same one
Outputs:
- coadd: float32 [32, 64, 512], P('patch', 'visit')
The draws below stay inside these ranges and needn't reach their ends.
Inputs may be any that keep to these rules, and one draw needn't show every extreme that they name: `tile_patch`: in the rows of one device no patch is named by more than 2 tiles, and every patch is named by some tile.
All inputs are finite; a program needn't handle non-finite values.
Results may differ from the reference program's by a relative error of at most 0.0057.
Values may be sent and summed in bfloat16 or wider, within the bound.
A program may use at most 128 MiB of HBM per device.

```python
import math
import jax
import jax.numpy as jnp
import numpy as np
from jax import lax

COLS = 512
ROWS = 64
TILES_DEV = 24
KHALF = 10
NBASIS = 40
NPATCHES = 32
CAPACITY = 2
TILES = 3072


def levels(key, extent, shards, least, high):
    def one(position, parts):
        steps = jax.random.uniform(jax.random.fold_in(jax.random.fold_in(key, 6), position), (parts,), jnp.float32, least / len(shards), high / len(shards))
        return jnp.repeat(jnp.exp(steps), extent[position] // parts).reshape((-1,) + (1,) * (len(extent) - position - 1))

    gain = one(*shards[0])
    for cut in shards[1:]:
        gain = gain * one(*cut)
    return gain


def routed_block(own_key, own, number, rows, amount, top, bound, skew):
    order = jax.random.permutation(own_key, amount)
    heavy_load, common = shares(amount, rows * top, bound, skew, True), shares(amount, rows * top, bound, skew, False)
    places = jnp.arange(amount)

    def named(sizes, turn):
        used = int((sizes > 0).sum())
        fixed = max(1, used // 4)
        shifted = fixed + (places - fixed + turn * (used - fixed)) % max(1, amount - fixed)
        return jnp.zeros((amount,), jnp.int32).at[order[jnp.where(places < fixed, places, shifted)]].set(jnp.asarray(sizes, jnp.int32))

    sizes = jnp.where(number % 4 == 0, named(heavy_load, number // 4), named(common, number - number // 4 - 1))
    mixed = jax.random.permutation(jax.random.fold_in(own, 3), amount)
    source_of, receiver = mixed[0:amount // 2 * 2:2], mixed[1:amount // 2 * 2:2]
    margin = jnp.minimum(sizes[source_of] - 1, bound - sizes[receiver]) // 2
    margin = jnp.where((source_of == order[0]) | (receiver == order[0]) | (sizes[receiver] == 0), 0, jnp.maximum(margin, 0))
    shifted = jax.random.randint(jax.random.fold_in(own, 4), (amount // 2,), 0, 1 << 20) % (margin + 1)
    sizes = sizes.at[source_of].add(-shifted).at[receiver].add(shifted)
    members = jnp.searchsorted(jnp.cumsum(sizes), jnp.arange(rows * top), side="right").astype(jnp.int32)
    listing = members.reshape(top, rows).T
    listing = listing[jax.random.permutation(jax.random.fold_in(own, 1), rows)]
    turn = jax.random.randint(jax.random.fold_in(own, 2), (rows, 1), 0, top)
    return jnp.take_along_axis(listing, (jnp.arange(top)[None, :] + turn) % top, axis=1)


def shares(count, total, reach, lean, full):
    weights = [(1 << 20) // math.isqrt(standing ** lean) + 1 for standing in range(1, count + 1)]
    largest = reach if full else min(reach, max(-(-total // count), total * weights[0] // sum(weights)))
    least = 1 if total - largest >= count - 1 else 0
    holding, surplus = [largest] + [least] * (count - 1), total - largest - least * (count - 1)
    while surplus > 0:
        free = [i for i in range(1, count) if holding[i] < largest] or [i for i in range(1, count) if holding[i] < reach]
        mass, remaining = sum([weights[i] for i in free]), surplus
        for i in free:
            extra = min(reach - holding[i], max(1, remaining * weights[i] // mass), surplus)
            holding[i] = holding[i] + extra
            surplus = surplus - extra
    return np.array(holding)


def scatter_about(key, extent, width, reach, shards=(), held_as=jnp.bfloat16):
    loudness = levels(key, extent, shards, -0.22, 0.18) if shards else 1.0
    result = jax.random.normal(key, extent, jnp.float32) * width * loudness
    return jnp.minimum(jnp.maximum(result, -reach), reach).astype(held_as)


def setup_inputs(seed: int = 0) -> dict:
    seeds = jax.random.split(jax.random.key(seed), 5)
    warp_image = scatter_about(seeds[0], (TILES, ROWS + 2 * KHALF, COLS), 1.0, 6.0, ((0, 128),), jnp.float32)
    warp_variance = jnp.clip(jnp.exp(math.log(4.0) - 2.7725887 * jax.random.uniform(seeds[1], (TILES, ROWS, COLS), jnp.float32) ** levels(seeds[1], (TILES, ROWS, COLS), ((0, 128),), -0.2, 0.2)), 0.25, 4.0)
    kernel_coef = scatter_about(seeds[2], (TILES, NBASIS), 0.1, 0.6, ((0, 128),), jnp.float32)
    tile_patch_keys = jax.random.split(jax.random.fold_in(seeds[3], 1), TILES // TILES_DEV)
    tile_patch_turns = jax.random.permutation(jax.random.fold_in(seeds[3], 3), TILES // TILES_DEV)
    tile_patch = jax.vmap(lambda own, number: routed_block(jax.random.fold_in(seeds[3], 2), own, number, TILES_DEV, NPATCHES, 1, CAPACITY, 2))(tile_patch_keys, tile_patch_turns).reshape((TILES, 1))
    return {"warp_image": warp_image, "warp_variance": warp_variance, "kernel_coef": kernel_coef, "tile_patch": tile_patch}


def basis_table():
    offsets = jnp.arange(2 * KHALF + 1, dtype=jnp.float32) - float(KHALF)
    scaled = offsets / float(KHALF)
    basis_terms = []
    for spread_px, degree in ((1.0, 4), (2.5, 4), (5.0, 3)):
        profile = jnp.exp(-offsets * offsets / (2.0 * spread_px * spread_px))
        for power_a in range(degree + 1):
            for power_b in range(degree + 1 - power_a):
                basis_terms.append(jnp.outer(profile * scaled ** power_a, profile * scaled ** power_b))
    return jnp.stack(basis_terms)


def reference(warp_image, warp_variance, kernel_coef, tile_patch):
    basis_set = basis_table()
    block_count = warp_image.shape[0] // TILES_DEV
    patch_ids = jnp.arange(NPATCHES, dtype=jnp.int32)

    def one_block(carry, block_index):
        first = (block_index * TILES_DEV).astype(jnp.int32)
        images = lax.dynamic_slice_in_dim(warp_image, first, TILES_DEV, 0)
        variance = lax.dynamic_slice_in_dim(warp_variance, first, TILES_DEV, 0)
        coefs = lax.dynamic_slice_in_dim(kernel_coef, first, TILES_DEV, 0)
        targets = lax.dynamic_slice_in_dim(tile_patch, first, TILES_DEV, 0)[:, 0]
        kernels = jnp.einsum("tb,buv->tuv", coefs, basis_set, precision=lax.Precision.HIGHEST)
        kernel_power = jnp.mean(kernels * kernels, axis=(1, 2)) + 1e-6
        weight = (1.0 / (variance * kernel_power[:, None, None])).astype(jnp.bfloat16)
        image_half = lax.optimization_barrier(images.astype(jnp.bfloat16))
        kernel_taps = lax.optimization_barrier(kernels.astype(jnp.bfloat16))
        matched = lax.conv_general_dilated(
            image_half.astype(jnp.float32)[None], kernel_taps.astype(jnp.float32)[:, None],
            (1, 1), ((0, 0), (KHALF, KHALF)), feature_group_count=TILES_DEV,
            precision=lax.Precision.HIGHEST)[0].astype(jnp.bfloat16)
        onehot = (targets[:, None] == patch_ids[None, :]).astype(jnp.float32)
        weight_full = weight.astype(jnp.float32)
        numerator = jnp.einsum("tp,trc->prc", onehot, weight_full * matched.astype(jnp.float32), precision=lax.Precision.HIGHEST)
        denominator = jnp.einsum("tp,trc->prc", onehot, weight_full, precision=lax.Precision.HIGHEST)
        return (carry[0] + numerator, carry[1] + denominator), None

    start_sums = (jnp.zeros((NPATCHES, ROWS, COLS), jnp.float32), jnp.zeros((NPATCHES, ROWS, COLS), jnp.float32))
    totals, unused = lax.scan(one_block, start_sums, jnp.arange(block_count, dtype=jnp.int32))
    return totals[0] / totals[1]
```

```python
import functools

import jax
import jax.numpy as jnp
import numpy as np
from jax import lax
from jax.experimental import pallas as pl
from jax.experimental.pallas import tpu as pltpu
from jax.sharding import PartitionSpec as P

KHALF = 10
TAPS = 2 * KHALF + 1
T = 24
ROWS = 64
COLS = 512
NPATCH = 32
BLK = 88
NK = 14
KDIM = 1280
NC = 2
W = COLS // NC
CB = W // 128
UNITS = 2 * CB
G = 2
NG = T // G
HI = lax.Precision.HIGHEST
F32 = jnp.float32
BF16 = jnp.bfloat16
MESH = pl.DeviceIdType.MESH


def tables():
    offsets = np.arange(TAPS, dtype=np.float64) - KHALF
    scaled = offsets / KHALF
    functions, place, terms = [], {}, []
    levels = ((1.0, 4), (2.5, 4), (5.0, 3))
    for s, (spread, degree) in enumerate(levels):
        profile = np.exp(-offsets * offsets / (2.0 * spread * spread))
        for i in range(degree + 1):
            place[s, i] = len(functions)
            functions.append(profile * scaled**i)
    for s, (spread, degree) in enumerate(levels):
        for i in range(degree + 1):
            for j in range(degree + 1 - i):
                terms.append((place[s, i], place[s, j]))
    g = np.array(functions)
    basis = np.zeros((len(terms), 512))
    for b, (ia, jb) in enumerate(terms):
        basis[b, : TAPS * TAPS] = np.outer(g[ia], g[jb]).reshape(-1)
    q = np.linalg.qr(g.T)[0]
    q = q.astype(jnp.bfloat16).astype(np.float64)
    mix = np.linalg.lstsq(q, g.T, rcond=None)[0]
    horizontal = np.zeros((256, NK * 128))
    for k in range(NK):
        for c in range(128):
            horizontal[c : c + TAPS, k * 128 + c] = q[:, k]
    vertical = np.zeros((len(terms), KDIM))
    for b, (ia, jb) in enumerate(terms):
        for k in range(NK):
            vertical[b, k * BLK : k * BLK + TAPS] = g[ia] * mix[k, jb]
    return basis.astype(np.float32), horizontal.astype(jnp.bfloat16), vertical.astype(np.float32)


def prepare_tile(t, x_ref, p_ref, v_ref, v0_ref):
    x = jnp.concatenate([x_ref.at[j][pl.ds(t, 84, stride=T), :] for j in range(4)], axis=1)
    x = jnp.concatenate([x, jnp.zeros((BLK - 84, COLS), F32)], axis=0)
    x = jnp.concatenate([x, jnp.zeros((BLK, 128), F32)], axis=1)
    x = pltpu.roll(x, KHALF, 1)
    p = jnp.concatenate([x[:, 128 * j : 128 * j + 256] for j in range(4)], axis=0)
    p_ref[t] = p.astype(BF16)
    row = jnp.broadcast_to(v0_ref[pl.ds(t, 1), :], (ROWS, KDIM))
    v_ref[t] = pltpu.roll(row, 0, 1, stride=1, stride_axis=0).astype(BF16)


def filter_columns(first, ch, p_ref, h_ref, y_ref):
    rows = BLK * CB
    lhs = jnp.concatenate([p_ref[first + u, rows * ch : rows * ch + rows, :] for u in range(G)], axis=0)
    for m in range(NK // 2):
        r = jnp.dot(lhs, h_ref[:, 256 * m : 256 * m + 256], preferred_element_type=F32)
        for u in range(G):
            for b in range(CB):
                o = rows * u + BLK * b
                y = jnp.concatenate([r[o : o + BLK, :128], r[o : o + BLK, 128:]], axis=0)
                y_ref[u, 2 * BLK * m : 2 * BLK * m + 2 * BLK, 128 * b : 128 * b + 128] = y.astype(BF16)


def match_rows(first, ch, v_ref, y_ref, var_ref, kp_ref, sum_ref):
    for u in range(G):
        t = first + u
        matched = jnp.dot(v_ref[t], y_ref[u], preferred_element_type=F32)
        w = (1.0 / (var_ref[t, :, W * ch : W * ch + W] * kp_ref[t])).astype(BF16).astype(F32)
        sum_ref[0, t] = w * matched
        sum_ref[1, t] = w


def place_coefs(a):
    cx = jnp.where(a == 0, 16, jnp.where(a == 1, 1, 4))
    cy = jnp.where(a == 0, 4, jnp.where(a == 1, 16, 1))
    cz = jnp.where(a == 0, 1, jnp.where(a == 1, 4, 16))
    return cx, cy, cz


def kernel(
    x_hbm, var_hbm, c_ref, tp_ref, bp_ref, h_ref, a_ref, out_ref,
    x_ref, var_ref, p_ref, v_ref, v0_ref, ya, yb, kp_ref, sum_ref,
    iv_ref, idx_ref, d_ref, own_ref, rc_ref, r1_ref, s1_ref, r2_ref, s2_ref, r3_ref, fin_ref,
    sx, sv, si, cs, cr, s1s, s1r, s2s, s2r, s3s, s3r,
):
    me_x = lax.axis_index("visit")
    me_p = lax.axis_index("patch")
    core = lax.rem(me_p, 2)
    me_y = lax.rem(me_p // 2, 4)
    me_z = me_p // 8

    def device(x, y, z, k):
        return (x, z * 8 + y * 2 + k)

    sibling = device(me_x, me_y, me_z, 1 - core)

    cpx = [
        pltpu.make_async_copy(
            x_hbm.at[pl.ds(T * 14 * (i // 4), T * 14), pl.ds(128 * (i % 4), 128)],
            x_ref.at[i % 4, pl.ds(T * 14 * (i // 4), T * 14)], sx.at[i])
        for i in range(24)
    ]
    cpv = [pltpu.make_async_copy(var_hbm.at[t], var_ref.at[t], sv.at[t]) for t in range(T)]
    for cp in cpx + cpv:
        cp.start()

    barrier = pltpu.get_barrier_semaphore()
    pl.semaphore_signal(barrier, inc=1, device_id=sibling, device_id_type=MESH)
    for d in range(1, 4):
        for who in (
            device(lax.rem(me_x + d, 4), me_y, me_z, core),
            device(me_x, lax.rem(me_y + d, 4), me_z, core),
            device(me_x, me_y, lax.rem(me_z + d, 4), core),
        ):
            pl.semaphore_signal(barrier, inc=1, device_id=who, device_id_type=MESH)

    lane = lax.broadcasted_iota(jnp.int32, (8, 128), 1)
    one = jnp.full((8, 128), T, jnp.int32)
    two = one
    for t in range(T):
        hit = lane == tp_ref[0, t]
        two = jnp.where(hit, one, two)
        one = jnp.where(hit, t, one)
    iv_ref[0:8, :] = one
    iv_ref[8:16, :] = two
    cpi = pltpu.make_async_copy(iv_ref, idx_ref, si)
    cpi.start()

    c = c_ref[...]
    taps = jnp.dot(c, bp_ref[...], precision=HI, preferred_element_type=F32)
    kp = jnp.sum(taps * taps, axis=1, keepdims=True) / float(TAPS * TAPS) + 1e-6
    for t in range(T):
        kp_ref[t] = jnp.broadcast_to(kp[t : t + 1], (1, W))
    v0_ref[...] = jnp.dot(c, a_ref[...], precision=HI, preferred_element_type=F32)
    for y in (ya, yb):
        for u in range(G):
            y[u, NK * BLK :, :] = jnp.zeros((KDIM - NK * BLK, W), BF16)
    for nd in range(2):
        sum_ref[nd, T] = jnp.zeros((ROWS, W), F32)
    for cp in cpx:
        cp.wait()

    def prepare(t, carry):
        prepare_tile(t, x_ref, p_ref, v_ref, v0_ref)
        return carry

    lax.fori_loop(0, T, prepare, 0)
    for cp in cpv:
        cp.wait()
    cpi.wait()

    def axis_of(u, k):
        return lax.rem(u + k, 3)

    def along(a, step, d):
        b = lax.rem(a + step, 3)
        here = jnp.where(b == 0, me_x, jnp.where(b == 1, me_y, me_z))
        there = lax.rem(here + d, 4)
        who = device(
            jnp.where(b == 0, there, me_x), jnp.where(b == 1, there, me_y), jnp.where(b == 2, there, me_z), core)
        return here, there, who

    def gather(k, store):
        def body(i, carry):
            z, y = i // 4, lax.rem(i, 4)
            p = z * 8 + y * 2 + k
            i1, i2 = idx_ref[0, p], idx_ref[8, p]
            for nd in range(2):
                s = sum_ref[nd, i1] + sum_ref[nd, i2]
                for cb in range(CB):
                    u = nd * CB + cb
                    cx, cy, cz = place_coefs(axis_of(u, k))
                    for x in range(4):
                        store(u, cx * x + cy * y + cz * z, s[16 * x : 16 * x + 16, 128 * cb : 128 * cb + 128])
            return carry
        lax.fori_loop(0, 16, body, 0)

    def core_copy(ch, u):
        return pltpu.make_async_remote_copy(
            src_ref=d_ref.at[ch, u], dst_ref=rc_ref.at[ch, u], send_sem=cs.at[ch, u], recv_sem=cr.at[ch, u],
            device_id=sibling, device_id_type=MESH)

    def copy1(ch, u, d):
        here, there, who = along(axis_of(u, core), 0, d)
        return pltpu.make_async_remote_copy(
            src_ref=rc_ref.at[ch, u, pl.ds(there * 16, 16)], dst_ref=r1_ref.at[ch, u, d - 1],
            send_sem=s1s.at[ch, u, d - 1], recv_sem=s1r.at[ch, u, d - 1], device_id=who, device_id_type=MESH)

    def copy2(ch, u, d):
        here, there, who = along(axis_of(u, core), 1, d)
        return pltpu.make_async_remote_copy(
            src_ref=s1_ref.at[ch, u, pl.ds(there * 4, 4)], dst_ref=r2_ref.at[ch, u, d - 1],
            send_sem=s2s.at[ch, u, d - 1], recv_sem=s2r.at[ch, u, d - 1], device_id=who, device_id_type=MESH)

    def copy3(ch, u, d):
        here, there, who = along(axis_of(u, core), 2, d)
        return pltpu.make_async_remote_copy(
            src_ref=s2_ref.at[ch, u, there], dst_ref=r3_ref.at[ch, u, d - 1],
            send_sem=s3s.at[ch, u, d - 1], recv_sem=s3r.at[ch, u, d - 1], device_id=who, device_id_type=MESH)

    def start_core(ch):
        def put(u, place, value):
            d_ref[ch, u, place] = value.astype(BF16)
        gather(1 - core, put)
        for u in range(UNITS):
            core_copy(ch, u).start()

        def keep(u, place, value):
            own_ref[u, place] = value
        gather(core, keep)

    def start_1(ch):
        for u in range(UNITS):
            core_copy(ch, u).wait_recv()

            def body(i, carry):
                at = pl.ds(i * 8, 8)
                rc_ref[ch, u, at] = (rc_ref[ch, u, at].astype(F32) + own_ref[u, at]).astype(BF16)
                return carry
            lax.fori_loop(0, 8, body, 0)
            for d in (2, 1, 3):
                copy1(ch, u, d).start()

    def start_2(ch):
        for u in range(UNITS):
            for d in range(1, 4):
                copy1(ch, u, d).wait_recv()
            here = along(axis_of(u, core), 0, 0)[0]
            total = rc_ref[ch, u, pl.ds(here * 16, 16)].astype(F32)
            for d in range(3):
                total = total + r1_ref[ch, u, d].astype(F32)
            s1_ref[ch, u] = total.astype(BF16)
            for d in (2, 1, 3):
                copy2(ch, u, d).start()

    def start_3(ch):
        for u in range(UNITS):
            for d in range(1, 4):
                copy2(ch, u, d).wait_recv()
            here = along(axis_of(u, core), 1, 0)[0]
            total = s1_ref[ch, u, pl.ds(here * 4, 4)].astype(F32)
            for d in range(3):
                total = total + r2_ref[ch, u, d].astype(F32)
            s2_ref[ch, u] = total
            for d in (2, 1, 3):
                copy3(ch, u, d).start()

    def finish(ch):
        for u in range(UNITS):
            for d in range(1, 4):
                copy3(ch, u, d).wait_recv()
            here = along(axis_of(u, core), 2, 0)[0]
            total = s2_ref[ch, u, here]
            for d in range(3):
                total = total + r3_ref[ch, u, d]
            fin_ref[u] = total
        for cb in range(CB):
            out_ref[:, W * ch + 128 * cb : W * ch + 128 * cb + 128] = fin_ref[cb] / fin_ref[CB + cb]

    def compute(ch, between):
        filter_columns(0, ch, p_ref, h_ref, ya)

        def body(i, carry):
            g = 2 * i
            filter_columns((g + 1) * G, ch, p_ref, h_ref, yb)
            match_rows(g * G, ch, v_ref, ya, var_ref, kp_ref, sum_ref)
            filter_columns((g + 2) * G, ch, p_ref, h_ref, ya)
            match_rows((g + 1) * G, ch, v_ref, yb, var_ref, kp_ref, sum_ref)
            for turn, step in between:
                pl.when(i == turn)(step)
            return carry

        lax.fori_loop(0, NG // 2 - 1, body, 0)
        filter_columns((NG - 1) * G, ch, p_ref, h_ref, yb)
        match_rows((NG - 2) * G, ch, v_ref, ya, var_ref, kp_ref, sum_ref)
        match_rows((NG - 1) * G, ch, v_ref, yb, var_ref, kp_ref, sum_ref)

    for ch in range(NC):
        if ch == 0:
            compute(ch, ())
            pl.semaphore_wait(barrier, 10)
        else:
            last = ch - 1
            compute(ch, (
                (1, functools.partial(start_1, last)),
                (3, functools.partial(start_2, last)),
                (4, functools.partial(start_3, last)),
            ))
        start_core(ch)
        if ch > 0:
            finish(ch - 1)
    last = NC - 1
    start_1(last)
    start_2(last)
    start_3(last)
    finish(last)

    for ch in range(NC):
        for u in range(UNITS):
            core_copy(ch, u).wait_send()
            for d in range(1, 4):
                copy1(ch, u, d).wait_send()
                copy2(ch, u, d).wait_send()
                copy3(ch, u, d).wait_send()


def on_device(warp_image, warp_variance, kernel_coef, tile_patch):
    basis, horizontal, vertical = tables()
    images = jnp.transpose(warp_image, (1, 0, 2)).reshape(84 * T, COLS)
    vmem = pl.BlockSpec(memory_space=pltpu.VMEM)
    smem = pl.BlockSpec(memory_space=pltpu.SMEM)
    hbm = pl.BlockSpec(memory_space=pl.ANY)
    dma = pltpu.SemaphoreType.DMA
    out = pl.pallas_call(
        kernel,
        out_shape=jax.ShapeDtypeStruct((ROWS // 4, COLS), F32),
        in_specs=[hbm, hbm, vmem, smem, vmem, vmem, vmem],
        out_specs=vmem,
        scratch_shapes=[
            pltpu.VMEM((4, 84 * T, 128), F32),
            pltpu.VMEM((T, ROWS, COLS), F32),
            pltpu.VMEM((T, 4 * BLK, 256), BF16),
            pltpu.VMEM((T, ROWS, KDIM), BF16),
            pltpu.VMEM((T, KDIM), F32),
            pltpu.VMEM((G, KDIM, W), BF16),
            pltpu.VMEM((G, KDIM, W), BF16),
            pltpu.VMEM((T, 1, W), F32),
            pltpu.VMEM((2, T + 1, ROWS, W), F32),
            pltpu.VMEM((16, 128), jnp.int32),
            pltpu.SMEM((16, 128), jnp.int32),
            pltpu.VMEM((NC, UNITS, 64, 16, 128), BF16),
            pltpu.VMEM((UNITS, 64, 16, 128), F32),
            pltpu.VMEM((NC, UNITS, 64, 16, 128), BF16),
            pltpu.VMEM((NC, UNITS, 3, 16, 16, 128), BF16),
            pltpu.VMEM((NC, UNITS, 16, 16, 128), BF16),
            pltpu.VMEM((NC, UNITS, 3, 4, 16, 128), BF16),
            pltpu.VMEM((NC, UNITS, 4, 16, 128), F32),
            pltpu.VMEM((NC, UNITS, 3, 16, 128), F32),
            pltpu.VMEM((UNITS, 16, 128), F32),
            dma((24,)), dma((T,)), dma,
            dma((NC, UNITS)), dma((NC, UNITS)),
            dma((NC, UNITS, 3)), dma((NC, UNITS, 3)),
            dma((NC, UNITS, 3)), dma((NC, UNITS, 3)),
            dma((NC, UNITS, 3)), dma((NC, UNITS, 3)),
        ],
        compiler_params=pltpu.CompilerParams(
            collective_id=0, has_side_effects=True, vmem_limit_bytes=60 * 2**20),
        name="coadd",
    )(images, warp_variance, kernel_coef, tile_patch.reshape(1, T),
      jnp.asarray(basis), jnp.asarray(horizontal), jnp.asarray(vertical))
    return out[None]


def solution(mesh):
    return jax.shard_map(
        on_device,
        mesh=mesh,
        in_specs=(
            P(("visit", "patch"), None, None),
            P(("visit", "patch"), None, None),
            P(("visit", "patch"), None),
            P(("visit", "patch"), None),
        ),
        out_specs=P("patch", "visit", None),
        check_vma=False,
    )
```

```python
import functools

import jax
import jax.numpy as jnp
import numpy as np
from jax import lax
from jax.experimental import pallas as pl
from jax.experimental.pallas import tpu as pltpu
from jax.sharding import PartitionSpec as P

KHALF = 10
TAPS = 2 * KHALF + 1
T = 24
ROWS = 64
COLS = 512
NPATCH = 32
BLK = 88
NK = 14
KDIM = 1280
NC = 2
W = COLS // NC
CB = W // 128
UNITS = 2 * CB
G = 2
NG = T // G
HI = lax.Precision.HIGHEST
F32 = jnp.float32
BF16 = jnp.bfloat16
MESH = pl.DeviceIdType.MESH


def tables():
    offsets = np.arange(TAPS, dtype=np.float64) - KHALF
    scaled = offsets / KHALF
    functions, place, terms = [], {}, []
    levels = ((1.0, 4), (2.5, 4), (5.0, 3))
    for s, (spread, degree) in enumerate(levels):
        profile = np.exp(-offsets * offsets / (2.0 * spread * spread))
        for i in range(degree + 1):
            place[s, i] = len(functions)
            functions.append(profile * scaled**i)
    for s, (spread, degree) in enumerate(levels):
        for i in range(degree + 1):
            for j in range(degree + 1 - i):
                terms.append((place[s, i], place[s, j]))
    g = np.array(functions)
    basis = np.zeros((len(terms), 512))
    for b, (ia, jb) in enumerate(terms):
        basis[b, : TAPS * TAPS] = np.outer(g[ia], g[jb]).reshape(-1)
    q = np.linalg.qr(g.T)[0]
    q = q.astype(jnp.bfloat16).astype(np.float64)
    mix = np.linalg.lstsq(q, g.T, rcond=None)[0]
    horizontal = np.zeros((256, NK * 128))
    for k in range(NK):
        for c in range(128):
            horizontal[c : c + TAPS, k * 128 + c] = q[:, k]
    vertical = np.zeros((len(terms), KDIM))
    for b, (ia, jb) in enumerate(terms):
        for k in range(NK):
            vertical[b, k * BLK : k * BLK + TAPS] = g[ia] * mix[k, jb]
    return basis.astype(np.float32), horizontal.astype(jnp.bfloat16), vertical.astype(np.float32)


def prepare_tile(t, x_ref, p_ref, v_ref, v0_ref):
    x = jnp.concatenate([x_ref.at[j][pl.ds(t, 84, stride=T), :] for j in range(4)], axis=1)
    x = jnp.concatenate([x, jnp.zeros((BLK - 84, COLS), F32)], axis=0)
    x = jnp.concatenate([x, jnp.zeros((BLK, 128), F32)], axis=1)
    x = pltpu.roll(x, KHALF, 1)
    p = jnp.concatenate([x[:, 128 * j : 128 * j + 256] for j in range(4)], axis=0)
    p_ref[t] = p.astype(BF16)
    row = jnp.broadcast_to(v0_ref[pl.ds(t, 1), :], (ROWS, KDIM))
    v_ref[t] = pltpu.roll(row, 0, 1, stride=1, stride_axis=0).astype(BF16)


def filter_columns(first, ch, p_ref, h_ref, y_ref):
    rows = BLK * CB
    lhs = jnp.concatenate([p_ref[first + u, rows * ch : rows * ch + rows, :] for u in range(G)], axis=0)
    for m in range(NK // 2):
        r = jnp.dot(lhs, h_ref[:, 256 * m : 256 * m + 256], preferred_element_type=F32)
        for u in range(G):
            for b in range(CB):
                o = rows * u + BLK * b
                y = jnp.concatenate([r[o : o + BLK, :128], r[o : o + BLK, 128:]], axis=0)
                y_ref[u, 2 * BLK * m : 2 * BLK * m + 2 * BLK, 128 * b : 128 * b + 128] = y.astype(BF16)


def match_rows(first, ch, v_ref, y_ref, var_ref, kp_ref, sum_ref):
    for u in range(G):
        t = first + u
        matched = jnp.dot(v_ref[t], y_ref[u], preferred_element_type=F32)
        w = (1.0 / (var_ref[t, :, W * ch : W * ch + W] * kp_ref[t])).astype(BF16).astype(F32)
        sum_ref[0, t] = w * matched
        sum_ref[1, t] = w


def place_coefs(a):
    cx = jnp.where(a == 0, 16, jnp.where(a == 1, 1, 4))
    cy = jnp.where(a == 0, 4, jnp.where(a == 1, 16, 1))
    cz = jnp.where(a == 0, 1, jnp.where(a == 1, 4, 16))
    return cx, cy, cz


def kernel(
    x_hbm, var_hbm, c_ref, tp_ref, bp_ref, h_ref, a_ref, out_ref,
    x_ref, var_ref, p_ref, v_ref, v0_ref, ya, yb, kp_ref, sum_ref,
    iv_ref, idx_ref, d_ref, own_ref, rc_ref, r1_ref, s1_ref, r2_ref, fin_ref,
    sx, sv, si, cs, cr, s1s, s1r, s2s, s2r,
):
    me_x = lax.axis_index("visit")
    me_p = lax.axis_index("patch")
    core = lax.rem(me_p, 2)
    me_y = lax.rem(me_p // 2, 4)
    me_z = me_p // 8

    def device(x, y, z, k):
        return (x, z * 8 + y * 2 + k)

    sibling = device(me_x, me_y, me_z, 1 - core)

    cpx = [
        pltpu.make_async_copy(
            x_hbm.at[pl.ds(T * 14 * (i // 4), T * 14), pl.ds(128 * (i % 4), 128)],
            x_ref.at[i % 4, pl.ds(T * 14 * (i // 4), T * 14)], sx.at[i])
        for i in range(24)
    ]
    cpv = [pltpu.make_async_copy(var_hbm.at[t], var_ref.at[t], sv.at[t]) for t in range(T)]
    for cp in cpx + cpv:
        cp.start()

    barrier = pltpu.get_barrier_semaphore()
    pl.semaphore_signal(barrier, inc=1, device_id=sibling, device_id_type=MESH)
    for d in range(1, 4):
        for who in (
            device(lax.rem(me_x + d, 4), me_y, me_z, core),
            device(me_x, lax.rem(me_y + d, 4), me_z, core),
            device(me_x, me_y, lax.rem(me_z + d, 4), core),
        ):
            pl.semaphore_signal(barrier, inc=1, device_id=who, device_id_type=MESH)
        for e in range(1, 4):
            for who in (
                device(lax.rem(me_x + d, 4), lax.rem(me_y + e, 4), me_z, core),
                device(me_x, lax.rem(me_y + d, 4), lax.rem(me_z + e, 4), core),
                device(lax.rem(me_x + d, 4), me_y, lax.rem(me_z + e, 4), core),
            ):
                pl.semaphore_signal(barrier, inc=1, device_id=who, device_id_type=MESH)

    lane = lax.broadcasted_iota(jnp.int32, (8, 128), 1)
    one = jnp.full((8, 128), T, jnp.int32)
    two = one
    for t in range(T):
        hit = lane == tp_ref[0, t]
        two = jnp.where(hit, one, two)
        one = jnp.where(hit, t, one)
    iv_ref[0:8, :] = one
    iv_ref[8:16, :] = two
    cpi = pltpu.make_async_copy(iv_ref, idx_ref, si)
    cpi.start()

    c = c_ref[...]
    taps = jnp.dot(c, bp_ref[...], precision=HI, preferred_element_type=F32)
    kp = jnp.sum(taps * taps, axis=1, keepdims=True) / float(TAPS * TAPS) + 1e-6
    for t in range(T):
        kp_ref[t] = jnp.broadcast_to(kp[t : t + 1], (1, W))
    v0_ref[...] = jnp.dot(c, a_ref[...], precision=HI, preferred_element_type=F32)
    for y in (ya, yb):
        for u in range(G):
            y[u, NK * BLK :, :] = jnp.zeros((KDIM - NK * BLK, W), BF16)
    for nd in range(2):
        sum_ref[nd, T] = jnp.zeros((ROWS, W), F32)
    for cp in cpx:
        cp.wait()

    def prepare(t, carry):
        prepare_tile(t, x_ref, p_ref, v_ref, v0_ref)
        return carry

    lax.fori_loop(0, T, prepare, 0)
    for cp in cpv:
        cp.wait()
    cpi.wait()

    def axis_of(u, k):
        return lax.rem(u + k, 3)

    def along(a, step, d):
        b = lax.rem(a + step, 3)
        here = jnp.where(b == 0, me_x, jnp.where(b == 1, me_y, me_z))
        there = lax.rem(here + d, 4)
        who = device(
            jnp.where(b == 0, there, me_x), jnp.where(b == 1, there, me_y), jnp.where(b == 2, there, me_z), core)
        return here, there, who

    def gather(k, store):
        def body(i, carry):
            z, y = i // 4, lax.rem(i, 4)
            p = z * 8 + y * 2 + k
            i1, i2 = idx_ref[0, p], idx_ref[8, p]
            for nd in range(2):
                s = sum_ref[nd, i1] + sum_ref[nd, i2]
                for cb in range(CB):
                    u = nd * CB + cb
                    cx, cy, cz = place_coefs(axis_of(u, k))
                    for x in range(4):
                        store(u, cx * x + cy * y + cz * z, s[16 * x : 16 * x + 16, 128 * cb : 128 * cb + 128])
            return carry
        lax.fori_loop(0, 16, body, 0)

    def core_copy(ch, u):
        return pltpu.make_async_remote_copy(
            src_ref=d_ref.at[ch, u], dst_ref=rc_ref.at[ch, u], send_sem=cs.at[ch, u], recv_sem=cr.at[ch, u],
            device_id=sibling, device_id_type=MESH)

    def copy1(ch, u, d):
        here, there, who = along(axis_of(u, core), 0, d)
        return pltpu.make_async_remote_copy(
            src_ref=rc_ref.at[ch, u, pl.ds(there * 16, 16)], dst_ref=r1_ref.at[ch, u, d - 1],
            send_sem=s1s.at[ch, u], recv_sem=s1r.at[ch, u], device_id=who, device_id_type=MESH)

    def copy2(ch, u, d):
        a = axis_of(u, core)
        there2, who2 = along(a, 1, d // 4)[1:]
        there3 = along(a, 2, d % 4)[1]
        b2, b3 = lax.rem(a + 1, 3), lax.rem(a + 2, 3)
        x = jnp.where(b2 == 0, there2, jnp.where(b3 == 0, there3, me_x))
        y = jnp.where(b2 == 1, there2, jnp.where(b3 == 1, there3, me_y))
        z = jnp.where(b2 == 2, there2, jnp.where(b3 == 2, there3, me_z))
        return pltpu.make_async_remote_copy(
            src_ref=s1_ref.at[ch, u, there2 * 4 + there3], dst_ref=r2_ref.at[ch, u, d - 1],
            send_sem=s2s.at[ch, u], recv_sem=s2r.at[ch, u], device_id=device(x, y, z, core), device_id_type=MESH)

    def settle(ref, sem):
        pltpu.make_async_copy(ref, ref, sem).wait()

    def start_core(ch):
        def put(u, place, value):
            d_ref[ch, u, place] = value.astype(BF16)
        gather(1 - core, put)
        for u in range(UNITS):
            core_copy(ch, u).start()

        def keep(u, place, value):
            own_ref[u, place] = value
        gather(core, keep)

    def start_1(ch):
        for u in range(UNITS):
            core_copy(ch, u).wait_recv()

            def body(i, carry):
                at = pl.ds(i * 8, 8)
                rc_ref[ch, u, at] = (rc_ref[ch, u, at].astype(F32) + own_ref[u, at]).astype(BF16)
                return carry
            lax.fori_loop(0, 8, body, 0)
            for d in (2, 1, 3):
                copy1(ch, u, d).start()

    def start_2(ch):
        for u in range(UNITS):
            settle(r1_ref.at[ch, u], s1r.at[ch, u])
            here = along(axis_of(u, core), 0, 0)[0]
            total = rc_ref[ch, u, pl.ds(here * 16, 16)].astype(F32)
            for d in range(3):
                total = total + r1_ref[ch, u, d].astype(F32)
            s1_ref[ch, u] = total.astype(BF16)
            for d in range(1, 16):
                copy2(ch, u, d).start()

    def finish(ch):
        for u in range(UNITS):
            settle(r2_ref.at[ch, u], s2r.at[ch, u])
            a = axis_of(u, core)
            total = s1_ref[ch, u, along(a, 1, 0)[0] * 4 + along(a, 2, 0)[0]].astype(F32)
            for d in range(15):
                total = total + r2_ref[ch, u, d].astype(F32)
            fin_ref[u] = total
        for cb in range(CB):
            out_ref[:, W * ch + 128 * cb : W * ch + 128 * cb + 128] = fin_ref[cb] / fin_ref[CB + cb]

    def compute(ch, between):
        filter_columns(0, ch, p_ref, h_ref, ya)

        def body(i, carry):
            g = 2 * i
            filter_columns((g + 1) * G, ch, p_ref, h_ref, yb)
            match_rows(g * G, ch, v_ref, ya, var_ref, kp_ref, sum_ref)
            filter_columns((g + 2) * G, ch, p_ref, h_ref, ya)
            match_rows((g + 1) * G, ch, v_ref, yb, var_ref, kp_ref, sum_ref)
            for turn, step in between:
                pl.when(i == turn)(step)
            return carry

        lax.fori_loop(0, NG // 2 - 1, body, 0)
        filter_columns((NG - 1) * G, ch, p_ref, h_ref, yb)
        match_rows((NG - 2) * G, ch, v_ref, ya, var_ref, kp_ref, sum_ref)
        match_rows((NG - 1) * G, ch, v_ref, yb, var_ref, kp_ref, sum_ref)

    compute(0, ())
    pl.semaphore_wait(barrier, 37)
    start_core(0)
    compute(1, ((1, functools.partial(start_1, 0)),))
    start_core(1)
    start_2(0)
    start_1(1)
    finish(0)
    start_2(1)
    finish(1)

    for ch in range(NC):
        for u in range(UNITS):
            core_copy(ch, u).wait_send()
            settle(r1_ref.at[ch, u], s1s.at[ch, u])
            settle(r2_ref.at[ch, u], s2s.at[ch, u])


def on_device(warp_image, warp_variance, kernel_coef, tile_patch):
    basis, horizontal, vertical = tables()
    images = jnp.transpose(warp_image, (1, 0, 2)).reshape(84 * T, COLS)
    vmem = pl.BlockSpec(memory_space=pltpu.VMEM)
    smem = pl.BlockSpec(memory_space=pltpu.SMEM)
    hbm = pl.BlockSpec(memory_space=pl.ANY)
    dma = pltpu.SemaphoreType.DMA
    out = pl.pallas_call(
        kernel,
        out_shape=jax.ShapeDtypeStruct((ROWS // 4, COLS), F32),
        in_specs=[hbm, hbm, vmem, smem, vmem, vmem, vmem],
        out_specs=vmem,
        scratch_shapes=[
            pltpu.VMEM((4, 84 * T, 128), F32),
            pltpu.VMEM((T, ROWS, COLS), F32),
            pltpu.VMEM((T, 4 * BLK, 256), BF16),
            pltpu.VMEM((T, ROWS, KDIM), BF16),
            pltpu.VMEM((T, KDIM), F32),
            pltpu.VMEM((G, KDIM, W), BF16),
            pltpu.VMEM((G, KDIM, W), BF16),
            pltpu.VMEM((T, 1, W), F32),
            pltpu.VMEM((2, T + 1, ROWS, W), F32),
            pltpu.VMEM((16, 128), jnp.int32),
            pltpu.SMEM((16, 128), jnp.int32),
            pltpu.VMEM((NC, UNITS, 64, 16, 128), BF16),
            pltpu.VMEM((UNITS, 64, 16, 128), F32),
            pltpu.VMEM((NC, UNITS, 64, 16, 128), BF16),
            pltpu.VMEM((NC, UNITS, 3, 16, 16, 128), BF16),
            pltpu.VMEM((NC, UNITS, 16, 16, 128), BF16),
            pltpu.VMEM((NC, UNITS, 15, 16, 128), BF16),
            pltpu.VMEM((UNITS, 16, 128), F32),
            dma((24,)), dma((T,)), dma,
            dma((NC, UNITS)), dma((NC, UNITS)),
            dma((NC, UNITS)), dma((NC, UNITS)),
            dma((NC, UNITS)), dma((NC, UNITS)),
        ],
        compiler_params=pltpu.CompilerParams(
            collective_id=0, has_side_effects=True, vmem_limit_bytes=60 * 2**20),
        name="coadd",
    )(images, warp_variance, kernel_coef, tile_patch.reshape(1, T),
      jnp.asarray(basis), jnp.asarray(horizontal), jnp.asarray(vertical))
    return out[None]


def solution(mesh):
    return jax.shard_map(
        on_device,
        mesh=mesh,
        in_specs=(
            P(("visit", "patch"), None, None),
            P(("visit", "patch"), None, None),
            P(("visit", "patch"), None),
            P(("visit", "patch"), None),
        ),
        out_specs=P("patch", "visit", None),
        check_vma=False,
    )
```

```python
import functools

import jax
import jax.numpy as jnp
import numpy as np
from jax import lax
from jax.experimental import pallas as pl
from jax.experimental.pallas import tpu as pltpu
from jax.sharding import PartitionSpec as P

KHALF = 10
TAPS = 2 * KHALF + 1
T = 24
ROWS = 64
COLS = 512
NPATCH = 32
BLK = 88
NK = 14
KDIM = 1280
CHUNKS = ((0, 2, 2), (2, 1, 4), (3, 1, 4))
PROWS = 368
PAT = (0, 88, 176, 272)
HI = lax.Precision.HIGHEST
F32 = jnp.float32
BF16 = jnp.bfloat16
MESH = pl.DeviceIdType.MESH


def tables():
    offsets = np.arange(TAPS, dtype=np.float64) - KHALF
    scaled = offsets / KHALF
    functions, place, terms = [], {}, []
    levels = ((1.0, 4), (2.5, 4), (5.0, 3))
    for s, (spread, degree) in enumerate(levels):
        profile = np.exp(-offsets * offsets / (2.0 * spread * spread))
        for i in range(degree + 1):
            place[s, i] = len(functions)
            functions.append(profile * scaled**i)
    for s, (spread, degree) in enumerate(levels):
        for i in range(degree + 1):
            for j in range(degree + 1 - i):
                terms.append((place[s, i], place[s, j]))
    g = np.array(functions)
    basis = np.zeros((len(terms), 512))
    for b, (ia, jb) in enumerate(terms):
        basis[b, : TAPS * TAPS] = np.outer(g[ia], g[jb]).reshape(-1)
    q = np.linalg.qr(g.T)[0]
    q = q.astype(jnp.bfloat16).astype(np.float64)
    mix = np.linalg.lstsq(q, g.T, rcond=None)[0]
    horizontal = np.zeros((256, NK * 128))
    for k in range(NK):
        for c in range(128):
            horizontal[c : c + TAPS, k * 128 + c] = q[:, k]
    vertical = np.zeros((len(terms), KDIM))
    for b, (ia, jb) in enumerate(terms):
        for k in range(NK):
            vertical[b, k * BLK : k * BLK + TAPS] = g[ia] * mix[k, jb]
    return basis.astype(np.float32), horizontal.astype(jnp.bfloat16), vertical.astype(np.float32)


def prepare_image(t, slot, x_ref, p_ref):
    x = jnp.concatenate([x_ref.at[j][pl.ds(t, 84, stride=T), :] for j in range(4)], axis=1)
    x = jnp.concatenate([x, jnp.zeros((BLK - 84, COLS), F32)], axis=0)
    x = jnp.concatenate([x, jnp.zeros((BLK, 128), F32)], axis=1)
    x = pltpu.roll(x, KHALF, 1)
    blocks = [x[:, 128 * j : 128 * j + 256] for j in range(4)]
    blocks.insert(3, jnp.zeros((8, 256), F32))
    blocks.append(jnp.zeros((8, 256), F32))
    p_ref[slot] = jnp.concatenate(blocks, axis=0).astype(BF16)


def prepare_band(t, slot, v_ref, v0_ref):
    row = jnp.broadcast_to(v0_ref[pl.ds(t, 1), :], (ROWS, KDIM))
    v_ref[slot] = pltpu.roll(row, 0, 1, stride=1, stride_axis=0).astype(BF16)


def filter_columns(first, group, block, cb, p_ref, h_ref, y_ref):
    rows = BLK * cb
    lhs = jnp.concatenate([p_ref[first + u, PAT[block] : PAT[block] + rows, :] for u in range(group)], axis=0)
    for m in range(NK // 2):
        r = jnp.dot(lhs, h_ref[:, 256 * m : 256 * m + 256], preferred_element_type=F32)
        for u in range(group):
            for b in range(cb):
                o = rows * u + BLK * b
                y = jnp.concatenate([r[o : o + BLK, :128], r[o : o + BLK, 128:]], axis=0)
                y_ref[u, 2 * BLK * m : 2 * BLK * m + 2 * BLK, 128 * b : 128 * b + 128] = y.astype(BF16)


def match_rows(tiles, first, group, block, cb, v_ref, y_ref, var_ref, kp_ref, sum_ref):
    cols = slice(128 * block, 128 * block + 128 * cb)
    for u in range(group):
        t = tiles + 4 * (u // 2) + u % 2
        matched = jnp.dot(v_ref[first + u], y_ref[u], preferred_element_type=F32)
        w = (1.0 / (var_ref[t, :, cols] * kp_ref[t][:, : 128 * cb])).astype(BF16).astype(F32)
        sum_ref[0, t, :, : 128 * cb] = w * matched
        sum_ref[1, t, :, : 128 * cb] = w


def place_coefs(a):
    cx = jnp.where(a == 0, 16, jnp.where(a == 1, 1, 4))
    cy = jnp.where(a == 0, 4, jnp.where(a == 1, 16, 1))
    cz = jnp.where(a == 0, 1, jnp.where(a == 1, 4, 16))
    return cx, cy, cz


def kernel(
    x_hbm, var_hbm, c_ref, tp_ref, bp_ref, h_hbm, a_ref, out_ref,
    x_ref, var_ref, h_ref, pe, po, ve, vo, v0_ref, ya2, yb2, ya1, yb1, kp_ref, sum_ref,
    iv_ref, idx_ref, own_ref, *rest,
):
    n = len(CHUNKS)
    m = n - 1
    dl_ref, ol_ref, rl_ref, el_ref = rest[5 * m : 5 * m + 4]
    sx, sv, si, sh, cs, cr, s1s, s1r, s2s, s2r, cls, clr, els, elr = rest[5 * m + 4 :]
    d_refs, rc_refs, r1_refs, s1_refs, r2_refs = (rest[i * m : i * m + m] for i in range(5))
    me_x = lax.axis_index("visit")
    me_p = lax.axis_index("patch")
    core = lax.rem(me_p, 2)
    me_y = lax.rem(me_p // 2, 4)
    me_z = me_p // 8

    def device(x, y, z, k):
        return (x, z * 8 + y * 2 + k)

    sibling = device(me_x, me_y, me_z, 1 - core)

    cpx = [
        pltpu.make_async_copy(
            x_hbm.at[pl.ds(T * 14 * (i // 4), T * 14), pl.ds(128 * (i % 4), 128)],
            x_ref.at[i % 4, pl.ds(T * 14 * (i // 4), T * 14)], sx.at[i])
        for i in range(24)
    ]
    cpv = [pltpu.make_async_copy(var_hbm.at[t], var_ref.at[t], sv.at[t]) for t in range(T)]
    cph = pltpu.make_async_copy(h_hbm, h_ref, sh)
    for cp in cpx + [cph] + cpv:
        cp.start()

    barrier = pltpu.get_barrier_semaphore()
    pl.semaphore_signal(barrier, inc=1, device_id=sibling, device_id_type=MESH)
    for d in range(1, 64):
        who = device(lax.rem(me_x + d // 4 % 4, 4), lax.rem(me_y + d % 4, 4), lax.rem(me_z + d // 16, 4), core)
        pl.semaphore_signal(barrier, inc=1, device_id=who, device_id_type=MESH)

    lane = lax.broadcasted_iota(jnp.int32, (8, 128), 1)
    one = jnp.full((8, 128), T, jnp.int32)
    two = one
    for t in range(T):
        hit = lane == tp_ref[0, t]
        two = jnp.where(hit, one, two)
        one = jnp.where(hit, t, one)
    iv_ref[0:8, :] = one
    iv_ref[8:16, :] = two
    cpi = pltpu.make_async_copy(iv_ref, idx_ref, si)
    cpi.start()

    c = c_ref[...]
    taps = jnp.dot(c, bp_ref[...], precision=HI, preferred_element_type=F32)
    kp = jnp.sum(taps * taps, axis=1, keepdims=True) / float(TAPS * TAPS) + 1e-6
    for t in range(T):
        kp_ref[t] = jnp.broadcast_to(kp[t : t + 1], (1, 256))
    v0_ref[...] = jnp.dot(c, a_ref[...], precision=HI, preferred_element_type=F32)
    for y in (ya2, yb2, ya1, yb1):
        for u in range(y.shape[0]):
            y[u, NK * BLK :, :] = jnp.zeros((KDIM - NK * BLK, y.shape[2]), BF16)
    for nd in range(2):
        sum_ref[nd, T] = jnp.zeros((ROWS, 256), F32)
    for cp in cpx:
        cp.wait()
    cph.wait()
    cpi.wait()

    def axis_of(ch, u, k):
        return lax.rem(u + k + ch, 3)

    def ring(b):
        here = jnp.where(b == 0, me_x, jnp.where(b == 1, me_y, me_z))
        to_v = jnp.where(b == 0, 1, 0)
        to_p = jnp.where(b == 0, 0, jnp.where(b == 1, 2, 8))
        places = [here] + [lax.rem(here + d, 4) for d in range(1, 4)]
        return [(at, (at - here) * to_v, (at - here) * to_p) for at in places]

    def units(ch):
        return CHUNKS[ch][1]

    def gather(ch, k, store):
        cbs = CHUNKS[ch][1]

        def body(i, carry):
            z, y = i // 4, lax.rem(i, 4)
            p = z * 8 + y * 2 + k
            i1, i2 = idx_ref[0, p], idx_ref[8, p]
            for nd in range(2):
                s = sum_ref[nd, i1, :, : 128 * cbs] + sum_ref[nd, i2, :, : 128 * cbs]
                for u in range(cbs):
                    cx, cy, cz = place_coefs(axis_of(ch, u, k))
                    for x in range(4):
                        store(u, cx * x + cy * y + cz * z, nd, s[16 * x : 16 * x + 16, 128 * u : 128 * u + 128])
            return carry
        lax.fori_loop(0, 16, body, 0)

    def core_copy(ch, u):
        return pltpu.make_async_remote_copy(
            src_ref=d_refs[ch].at[u], dst_ref=rc_refs[ch].at[u], send_sem=cs.at[ch, u], recv_sem=cr.at[ch, u],
            device_id=sibling, device_id_type=MESH)

    def settle(ref, sem):
        pltpu.make_async_copy(ref, ref, sem).wait()

    def start_core(ch):
        def put(u, place, nd, value):
            d_refs[ch][u, place, nd] = value.astype(BF16)
        gather(ch, 1 - core, put)
        for u in range(units(ch)):
            core_copy(ch, u).start()

        def keep(u, place, nd, value):
            own_ref[u, place, nd] = value
        gather(ch, core, keep)

    def start_1(ch):
        for u in range(units(ch)):
            core_copy(ch, u).wait_recv()
            around = ring(axis_of(ch, u, core))

            def body(i, carry):
                at = pl.ds(i * 4, 4)
                rc_refs[ch][u, at] = (rc_refs[ch][u, at].astype(F32) + own_ref[u, at]).astype(BF16)
                return carry
            lax.fori_loop(0, 16, body, 0)
            for d in (2, 1, 3):
                there, v, p = around[d]
                pltpu.make_async_remote_copy(
                    src_ref=rc_refs[ch].at[u, pl.ds(there * 16, 16)], dst_ref=r1_refs[ch].at[u, d - 1],
                    send_sem=s1s.at[ch, u], recv_sem=s1r.at[ch, u],
                    device_id=(me_x + v, me_p + p), device_id_type=MESH).start()

    def start_2(ch):
        for u in range(units(ch)):
            a = axis_of(ch, u, core)
            here = ring(a)[0][0]
            second, third = ring(lax.rem(a + 1, 3)), ring(lax.rem(a + 2, 3))
            settle(r1_refs[ch].at[u], s1r.at[ch, u])
            total = rc_refs[ch][u, pl.ds(here * 16, 16)].astype(F32)
            for d in range(3):
                total = total + r1_refs[ch][u, d].astype(F32)
            s1_refs[ch][u] = total.astype(BF16)
            for d in (10, 6, 9, 11, 14, 2, 8, 5, 7, 13, 15, 1, 3, 4, 12):
                at2, v2, p2 = second[d // 4]
                at3, v3, p3 = third[d % 4]
                pltpu.make_async_remote_copy(
                    src_ref=s1_refs[ch].at[u, at2 * 4 + at3], dst_ref=r2_refs[ch].at[u, d - 1],
                    send_sem=s2s.at[ch, u], recv_sem=s2r.at[ch, u],
                    device_id=(me_x + v2 + v3, me_p + p2 + p3), device_id_type=MESH).start()

    def finish(ch):
        for u in range(units(ch)):
            a = axis_of(ch, u, core)
            here = ring(lax.rem(a + 1, 3))[0][0] * 4 + ring(lax.rem(a + 2, 3))[0][0]
            settle(r2_refs[ch].at[u], s2r.at[ch, u])
            total = s1_refs[ch][u, here].astype(F32)
            for d in range(15):
                total = total + r2_refs[ch][u, d].astype(F32)
            at = 128 * (CHUNKS[ch][0] + u)
            out_ref[:, at : at + 128] = total[0] / total[1]

    def last_gather(dz, k, store):
        z = lax.rem(me_z + dz, 4)

        def body(y, carry):
            p = z * 8 + y * 2 + k
            i1, i2 = idx_ref[0, p], idx_ref[8, p]
            for nd in range(2):
                s = sum_ref[nd, i1, :, :128] + sum_ref[nd, i2, :, :128]
                for x in range(4):
                    store(dz, x * 4 + y, nd, s[16 * x : 16 * x + 16])
            return carry
        lax.fori_loop(0, 4, body, 0)

    def last_copy(dz):
        return pltpu.make_async_remote_copy(
            src_ref=dl_ref.at[dz], dst_ref=rl_ref.at[dz], send_sem=cls.at[dz], recv_sem=clr.at[dz],
            device_id=sibling, device_id_type=MESH)

    def last_core():
        def put(dz, place, nd, value):
            dl_ref[dz, place, nd] = value.astype(BF16)

        def keep(dz, place, nd, value):
            ol_ref[dz, place, nd] = value
        for dz in (2, 1, 3, 0):
            last_gather(dz, 1 - core, put)
            last_copy(dz).start()
        for dz in (2, 1, 3, 0):
            last_gather(dz, core, keep)

    def last_spread():
        for dz in (2, 1, 3, 0):
            last_copy(dz).wait_recv()
            rl_ref[dz] = (rl_ref[dz].astype(F32) + ol_ref[dz]).astype(BF16)
            z = lax.rem(me_z + dz, 4)
            for dx in (2, 1, 3, 0):
                x = lax.rem(me_x + dx, 4)
                for dy in (2, 1, 3, 0):
                    y = lax.rem(me_y + dy, 4)
                    slot = dz * 16 + dx * 4 + dy - 1
                    if slot >= 0:
                        pltpu.make_async_remote_copy(
                            src_ref=rl_ref.at[dz, x * 4 + y], dst_ref=el_ref.at[slot], send_sem=els, recv_sem=elr,
                            device_id=device(x, y, z, core), device_id_type=MESH).start()

    def last_finish():
        settle(el_ref, elr)
        total = rl_ref[0, me_x * 4 + me_y].astype(F32)

        def body(i, total):
            for k in range(9):
                total = total + el_ref[i * 9 + k].astype(F32)
            return total
        total = lax.fori_loop(0, 7, body, total)
        out_ref[:, COLS - 128 :] = total[0] / total[1]

    def compute(ch, between):
        block, cb, group = CHUNKS[ch]
        ya, yb = (ya2, yb2) if cb == 2 else (ya1, yb1)
        ng = T // group

        def images(g, parity):
            for u in range(group):
                t = 2 * g * group + 2 * parity + u
                prepare_image(t, g * group + u, x_ref, (pe, po)[parity])

        def bands(g, parity):
            for u in range(group):
                t = 2 * g * group + 2 * parity + u
                prepare_band(t, g * group + u, (ve, vo)[parity], v0_ref)

        def where(g, parity):
            return (pe, po)[parity], (ve, vo)[parity], g * group, 2 * g * group + 2 * parity

        def filters(g, parity, y):
            p, v, slot, t = where(g, parity)
            filter_columns(slot, group, block, cb, p, h_ref, y)

        def matches(g, parity, y):
            p, v, slot, t = where(g, parity)
            match_rows(t, slot, group, block, cb, v, y, var_ref, kp_ref, sum_ref)

        if ch == 0:
            for g, parity in ((0, 0), (0, 1), (1, 0)):
                images(g, parity)
                bands(g, parity)
            for cp in cpv:
                cp.wait()
        filters(0, 0, ya)

        def body(i, carry):
            after = jnp.minimum(i + 2, ng // 2 - 1)
            filters(i, 1, yb)
            if ch == 0:
                images(i + 1, 1)
            matches(i, 0, ya)
            if ch == 0:
                bands(after, 0)
            filters(i + 1, 0, ya)
            if ch == 0:
                images(after, 0)
            matches(i, 1, yb)
            if ch == 0:
                bands(i + 1, 1)
            for turn, step in between:
                pl.when(i == turn)(step)
            return carry

        lax.fori_loop(0, ng // 2 - 1, body, 0)
        filters(ng // 2 - 1, 1, yb)
        matches(ng // 2 - 1, 0, ya)
        matches(ng // 2 - 1, 1, yb)

    compute(0, ())
    pl.semaphore_wait(barrier, 64)
    start_core(0)
    compute(1, ((0, functools.partial(start_1, 0)),))
    start_core(1)
    compute(2, ((0, functools.partial(start_1, 1)),))
    last_core()
    start_2(0)
    last_spread()
    start_2(1)
    finish(0)
    finish(1)
    last_finish()

    for dz in range(4):
        last_copy(dz).wait_send()
    settle(el_ref, els)
    for ch in range(n - 1):
        for u in range(units(ch)):
            core_copy(ch, u).wait_send()
            settle(r1_refs[ch].at[u], s1s.at[ch, u])
            settle(r2_refs[ch].at[u], s2s.at[ch, u])


def on_device(warp_image, warp_variance, kernel_coef, tile_patch):
    basis, horizontal, vertical = tables()
    images = jnp.transpose(warp_image, (1, 0, 2)).reshape(84 * T, COLS)
    vmem = pl.BlockSpec(memory_space=pltpu.VMEM)
    smem = pl.BlockSpec(memory_space=pltpu.SMEM)
    hbm = pl.BlockSpec(memory_space=pl.ANY)
    dma = pltpu.SemaphoreType.DMA
    units = [chunk[1] for chunk in CHUNKS[:-1]]
    out = pl.pallas_call(
        kernel,
        out_shape=jax.ShapeDtypeStruct((ROWS // 4, COLS), F32),
        in_specs=[hbm, hbm, vmem, smem, vmem, hbm, vmem],
        out_specs=vmem,
        scratch_shapes=[
            pltpu.VMEM((4, 84 * T, 128), F32),
            pltpu.VMEM((T, ROWS, COLS), F32),
            pltpu.VMEM((256, NK * 128), BF16),
            pltpu.VMEM((T // 2, PROWS, 256), BF16),
            pltpu.VMEM((T // 2, PROWS, 256), BF16),
            pltpu.VMEM((T // 2, ROWS, KDIM), BF16),
            pltpu.VMEM((T // 2, ROWS, KDIM), BF16),
            pltpu.VMEM((T, KDIM), F32),
            pltpu.VMEM((2, KDIM, 256), BF16),
            pltpu.VMEM((2, KDIM, 256), BF16),
            pltpu.VMEM((4, KDIM, 128), BF16),
            pltpu.VMEM((4, KDIM, 128), BF16),
            pltpu.VMEM((T, 1, 256), F32),
            pltpu.VMEM((2, T + 1, ROWS, 256), F32),
            pltpu.VMEM((16, 128), jnp.int32),
            pltpu.SMEM((16, 128), jnp.int32),
            pltpu.VMEM((2, 64, 2, 16, 128), F32),
            *[pltpu.VMEM((u, 64, 2, 16, 128), BF16) for u in units],
            *[pltpu.VMEM((u, 64, 2, 16, 128), BF16) for u in units],
            *[pltpu.VMEM((u, 3, 16, 2, 16, 128), BF16) for u in units],
            *[pltpu.VMEM((u, 16, 2, 16, 128), BF16) for u in units],
            *[pltpu.VMEM((u, 15, 2, 16, 128), BF16) for u in units],
            pltpu.VMEM((4, 16, 2, 16, 128), BF16),
            pltpu.VMEM((4, 16, 2, 16, 128), F32),
            pltpu.VMEM((4, 16, 2, 16, 128), BF16),
            pltpu.VMEM((63, 2, 16, 128), BF16),
            dma((24,)), dma((T,)), dma, dma,
            *[dma((len(units), 2))] * 6,
            dma((4,)), dma((4,)), dma, dma,
        ],
        compiler_params=pltpu.CompilerParams(
            collective_id=0, has_side_effects=True, vmem_limit_bytes=60 * 2**20),
        name="coadd",
    )(images, warp_variance, kernel_coef, tile_patch.reshape(1, T),
      jnp.asarray(basis), jnp.asarray(horizontal), jnp.asarray(vertical))
    return out[None]


def solution(mesh):
    return jax.shard_map(
        on_device,
        mesh=mesh,
        in_specs=(
            P(("visit", "patch"), None, None),
            P(("visit", "patch"), None, None),
            P(("visit", "patch"), None),
            P(("visit", "patch"), None),
        ),
        out_specs=P("patch", "visit", None),
        check_vma=False,
    )
```

```python
import functools

import jax
import jax.numpy as jnp
import numpy as np
from jax import lax
from jax.experimental import pallas as pl
from jax.experimental.pallas import tpu as pltpu
from jax.sharding import PartitionSpec as P

KHALF = 10
TAPS = 2 * KHALF + 1
T = 24
ROWS = 64
COLS = 512
NPATCH = 32
BLK = 88
NK = 14
KDIM = 1280
CHUNKS = ((0, 2, 2), (2, 1, 4), (3, 1, 4))
PROWS = 368
PAT = (0, 88, 176, 272)
HI = lax.Precision.HIGHEST
F32 = jnp.float32
BF16 = jnp.bfloat16
MESH = pl.DeviceIdType.MESH


def tables():
    offsets = np.arange(TAPS, dtype=np.float64) - KHALF
    scaled = offsets / KHALF
    functions, place, terms = [], {}, []
    levels = ((1.0, 4), (2.5, 4), (5.0, 3))
    for s, (spread, degree) in enumerate(levels):
        profile = np.exp(-offsets * offsets / (2.0 * spread * spread))
        for i in range(degree + 1):
            place[s, i] = len(functions)
            functions.append(profile * scaled**i)
    for s, (spread, degree) in enumerate(levels):
        for i in range(degree + 1):
            for j in range(degree + 1 - i):
                terms.append((place[s, i], place[s, j]))
    g = np.array(functions)
    basis = np.zeros((len(terms), 512))
    for b, (ia, jb) in enumerate(terms):
        basis[b, : TAPS * TAPS] = np.outer(g[ia], g[jb]).reshape(-1)
    q = np.linalg.qr(g.T)[0]
    q = q.astype(jnp.bfloat16).astype(np.float64)
    mix = np.linalg.lstsq(q, g.T, rcond=None)[0]
    horizontal = np.zeros((256, NK * 128))
    for k in range(NK):
        for c in range(128):
            horizontal[c : c + TAPS, k * 128 + c] = q[:, k]
    vertical = np.zeros((len(terms), KDIM))
    for b, (ia, jb) in enumerate(terms):
        for k in range(NK):
            vertical[b, k * BLK : k * BLK + TAPS] = g[ia] * mix[k, jb]
    return basis.astype(np.float32), horizontal.astype(jnp.bfloat16), vertical.astype(np.float32)


def prepare_image(t, slot, x_ref, p_ref):
    x = jnp.concatenate([x_ref.at[j][pl.ds(t, 84, stride=T), :] for j in range(4)], axis=1)
    x = jnp.concatenate([x, jnp.zeros((BLK - 84, COLS), F32)], axis=0)
    x = jnp.concatenate([x, jnp.zeros((BLK, 128), F32)], axis=1)
    x = pltpu.roll(x, KHALF, 1)
    blocks = [x[:, 128 * j : 128 * j + 256] for j in range(4)]
    blocks.insert(3, jnp.zeros((8, 256), F32))
    blocks.append(jnp.zeros((8, 256), F32))
    p_ref[slot] = jnp.concatenate(blocks, axis=0).astype(BF16)


def prepare_band(t, slot, v_ref, v0_ref):
    row = jnp.broadcast_to(v0_ref[pl.ds(t, 1), :], (ROWS, KDIM))
    v_ref[slot] = pltpu.roll(row, 0, 1, stride=1, stride_axis=0).astype(BF16)


def filter_columns(first, group, block, cb, p_ref, h_ref, y_ref):
    rows = BLK * cb
    lhs = jnp.concatenate([p_ref[first + u, PAT[block] : PAT[block] + rows, :] for u in range(group)], axis=0)
    for m in range(NK // 2):
        r = jnp.dot(lhs, h_ref[:, 256 * m : 256 * m + 256], preferred_element_type=F32)
        for u in range(group):
            for b in range(cb):
                o = rows * u + BLK * b
                y = jnp.concatenate([r[o : o + BLK, :128], r[o : o + BLK, 128:]], axis=0)
                y_ref[u, 2 * BLK * m : 2 * BLK * m + 2 * BLK, 128 * b : 128 * b + 128] = y.astype(BF16)


def match_rows(tiles, first, group, block, cb, v_ref, y_ref, var_ref, kp_ref, sum_ref):
    cols = slice(128 * block, 128 * block + 128 * cb)
    for u in range(group):
        t = tiles + 4 * (u // 2) + u % 2
        matched = jnp.dot(v_ref[first + u], y_ref[u], preferred_element_type=F32)
        w = (1.0 / (var_ref[t, :, cols] * kp_ref[t][:, : 128 * cb])).astype(BF16).astype(F32)
        sum_ref[0, t, :, : 128 * cb] = w * matched
        sum_ref[1, t, :, : 128 * cb] = w


def place_coefs(a):
    cx = jnp.where(a == 0, 16, jnp.where(a == 1, 1, 4))
    cy = jnp.where(a == 0, 4, jnp.where(a == 1, 16, 1))
    cz = jnp.where(a == 0, 1, jnp.where(a == 1, 4, 16))
    return cx, cy, cz


def kernel(
    x_hbm, var_hbm, c_ref, tp_ref, bp_ref, h_hbm, a_ref, out_ref,
    x_ref, var_ref, h_ref, pe, po, ve, vo, v0_ref, ya2, yb2, ya1, yb1, kp_ref, sum_ref,
    iv_ref, idx_ref, own_ref, *rest,
):
    n = len(CHUNKS)
    m = n - 1
    dl_ref, ol_ref, rl_ref, el_ref = rest[5 * m : 5 * m + 4]
    sx, sv, si, sh, cs, cr, s1s, s1r, s2s, s2r, cls, clr, els, elr = rest[5 * m + 4 :]
    d_refs, rc_refs, r1_refs, s1_refs, r2_refs = (rest[i * m : i * m + m] for i in range(5))
    me_x = lax.axis_index("visit")
    me_p = lax.axis_index("patch")
    core = lax.rem(me_p, 2)
    me_y = lax.rem(me_p // 2, 4)
    me_z = me_p // 8

    def device(x, y, z, k):
        return (x, z * 8 + y * 2 + k)

    sibling = device(me_x, me_y, me_z, 1 - core)

    cpx = [
        pltpu.make_async_copy(
            x_hbm.at[pl.ds(T * 14 * (i // 4), T * 14), pl.ds(128 * (i % 4), 128)],
            x_ref.at[i % 4, pl.ds(T * 14 * (i // 4), T * 14)], sx.at[i])
        for i in range(24)
    ]
    cpv = [pltpu.make_async_copy(var_hbm.at[t], var_ref.at[t], sv.at[t]) for t in range(T)]
    cph = pltpu.make_async_copy(h_hbm, h_ref, sh)
    for cp in cpx + [cph] + cpv:
        cp.start()

    barrier = pltpu.get_barrier_semaphore()
    pl.semaphore_signal(barrier, inc=1, device_id=sibling, device_id_type=MESH)
    for d in range(1, 64):
        who = device(lax.rem(me_x + d // 4 % 4, 4), lax.rem(me_y + d % 4, 4), lax.rem(me_z + d // 16, 4), core)
        pl.semaphore_signal(barrier, inc=1, device_id=who, device_id_type=MESH)

    lane = lax.broadcasted_iota(jnp.int32, (8, 128), 1)
    one = jnp.full((8, 128), T, jnp.int32)
    two = one
    for t in range(T):
        hit = lane == tp_ref[0, t]
        two = jnp.where(hit, one, two)
        one = jnp.where(hit, t, one)
    iv_ref[0:8, :] = one
    iv_ref[8:16, :] = two
    cpi = pltpu.make_async_copy(iv_ref, idx_ref, si)
    cpi.start()

    c = c_ref[...]
    taps = jnp.dot(c, bp_ref[...], precision=HI, preferred_element_type=F32)
    kp = jnp.sum(taps * taps, axis=1, keepdims=True) / float(TAPS * TAPS) + 1e-6
    for t in range(T):
        kp_ref[t] = jnp.broadcast_to(kp[t : t + 1], (1, 256))
    v0_ref[...] = jnp.dot(c, a_ref[...], precision=HI, preferred_element_type=F32)
    for y in (ya2, yb2, ya1, yb1):
        for u in range(y.shape[0]):
            y[u, NK * BLK :, :] = jnp.zeros((KDIM - NK * BLK, y.shape[2]), BF16)
    for nd in range(2):
        sum_ref[nd, T] = jnp.zeros((ROWS, 256), F32)
    for cp in cpx:
        cp.wait()
    cph.wait()
    cpi.wait()

    def axis_of(ch, u, k):
        return lax.rem(u + k + ch * k, 3)

    def ring(b):
        here = jnp.where(b == 0, me_x, jnp.where(b == 1, me_y, me_z))
        to_v = jnp.where(b == 0, 1, 0)
        to_p = jnp.where(b == 0, 0, jnp.where(b == 1, 2, 8))
        places = [here] + [lax.rem(here + d, 4) for d in range(1, 4)]
        return [(at, (at - here) * to_v, (at - here) * to_p) for at in places]

    def units(ch):
        return CHUNKS[ch][1]

    def gather(ch, k, store):
        cbs = CHUNKS[ch][1]

        def body(i, carry):
            z, y = i // 4, lax.rem(i, 4)
            p = z * 8 + y * 2 + k
            i1, i2 = idx_ref[0, p], idx_ref[8, p]
            for nd in range(2):
                s = sum_ref[nd, i1, :, : 128 * cbs] + sum_ref[nd, i2, :, : 128 * cbs]
                for u in range(cbs):
                    cx, cy, cz = place_coefs(axis_of(ch, u, k))
                    for x in range(4):
                        store(u, cx * x + cy * y + cz * z, nd, s[16 * x : 16 * x + 16, 128 * u : 128 * u + 128])
            return carry
        lax.fori_loop(0, 16, body, 0, unroll=4)

    def core_copy(ch, u):
        return pltpu.make_async_remote_copy(
            src_ref=d_refs[ch].at[u], dst_ref=rc_refs[ch].at[u], send_sem=cs.at[ch, u], recv_sem=cr.at[ch, u],
            device_id=sibling, device_id_type=MESH)

    def settle(ref, sem):
        pltpu.make_async_copy(ref, ref, sem).wait()

    def start_core(ch):
        def put(u, place, nd, value):
            d_refs[ch][u, place, nd] = value.astype(BF16)
        gather(ch, 1 - core, put)
        for u in range(units(ch)):
            core_copy(ch, u).start()

        def keep(u, place, nd, value):
            own_ref[u, place, nd] = value
        gather(ch, core, keep)

    def start_1(ch, some=None):
        for u in some or range(units(ch)):
            core_copy(ch, u).wait_recv()
            around = ring(axis_of(ch, u, core))

            def body(i, carry):
                at = pl.ds(i * 4, 4)
                rc_refs[ch][u, at] = (rc_refs[ch][u, at].astype(F32) + own_ref[u, at]).astype(BF16)
                return carry
            lax.fori_loop(0, 16, body, 0)
            for d in (2, 1, 3):
                there, v, p = around[d]
                pltpu.make_async_remote_copy(
                    src_ref=rc_refs[ch].at[u, pl.ds(there * 16, 16)], dst_ref=r1_refs[ch].at[u, d - 1],
                    send_sem=s1s.at[ch, u], recv_sem=s1r.at[ch, u],
                    device_id=(me_x + v, me_p + p), device_id_type=MESH).start()

    def start_2(ch):
        for u in range(units(ch)):
            a = axis_of(ch, u, core)
            here = ring(a)[0][0]
            second, third = ring(lax.rem(a + 1, 3)), ring(lax.rem(a + 2, 3))
            settle(r1_refs[ch].at[u], s1r.at[ch, u])
            total = rc_refs[ch][u, pl.ds(here * 16, 16)].astype(F32)
            for d in range(3):
                total = total + r1_refs[ch][u, d].astype(F32)
            s1_refs[ch][u] = total.astype(BF16)
            for d in (10, 6, 9, 11, 14, 2, 8, 5, 7, 13, 15, 1, 3, 4, 12):
                at2, v2, p2 = second[d // 4]
                at3, v3, p3 = third[d % 4]
                pltpu.make_async_remote_copy(
                    src_ref=s1_refs[ch].at[u, at2 * 4 + at3], dst_ref=r2_refs[ch].at[u, d - 1],
                    send_sem=s2s.at[ch, u], recv_sem=s2r.at[ch, u],
                    device_id=(me_x + v2 + v3, me_p + p2 + p3), device_id_type=MESH).start()

    def finish(ch):
        for u in range(units(ch)):
            a = axis_of(ch, u, core)
            here = ring(lax.rem(a + 1, 3))[0][0] * 4 + ring(lax.rem(a + 2, 3))[0][0]
            settle(r2_refs[ch].at[u], s2r.at[ch, u])
            total = s1_refs[ch][u, here].astype(F32)
            for d in range(15):
                total = total + r2_refs[ch][u, d].astype(F32)
            at = 128 * (CHUNKS[ch][0] + u)
            out_ref[:, at : at + 128] = total[0] / total[1]

    def last_gather(dz, k, store):
        z = lax.rem(me_z + dz, 4)

        def body(y, carry):
            p = z * 8 + y * 2 + k
            i1, i2 = idx_ref[0, p], idx_ref[8, p]
            for nd in range(2):
                s = sum_ref[nd, i1, :, :128] + sum_ref[nd, i2, :, :128]
                for x in range(4):
                    store(dz, x * 4 + y, nd, s[16 * x : 16 * x + 16])
            return carry
        lax.fori_loop(0, 4, body, 0, unroll=4)

    def last_copy(dz):
        return pltpu.make_async_remote_copy(
            src_ref=dl_ref.at[dz], dst_ref=rl_ref.at[dz], send_sem=cls.at[dz], recv_sem=clr.at[dz],
            device_id=sibling, device_id_type=MESH)

    def last_core():
        def put(dz, place, nd, value):
            dl_ref[dz, place, nd] = value.astype(BF16)

        def keep(dz, place, nd, value):
            ol_ref[dz, place, nd] = value
        for dz in (2, 1, 3, 0):
            last_gather(dz, 1 - core, put)
            last_copy(dz).start()
        for dz in (2, 1, 3, 0):
            last_gather(dz, core, keep)

    def last_spread():
        for dz in (2, 1, 3, 0):
            last_copy(dz).wait_recv()
            rl_ref[dz] = (rl_ref[dz].astype(F32) + ol_ref[dz]).astype(BF16)
            z = lax.rem(me_z + dz, 4)
            for dx in (2, 1, 3, 0):
                x = lax.rem(me_x + dx, 4)
                for dy in (2, 1, 3, 0):
                    y = lax.rem(me_y + dy, 4)
                    slot = dz * 16 + dx * 4 + dy - 1
                    if slot >= 0:
                        pltpu.make_async_remote_copy(
                            src_ref=rl_ref.at[dz, x * 4 + y], dst_ref=el_ref.at[slot], send_sem=els, recv_sem=elr,
                            device_id=device(x, y, z, core), device_id_type=MESH).start()

    def last_finish():
        settle(el_ref, elr)
        total = rl_ref[0, me_x * 4 + me_y].astype(F32)

        def body(i, total):
            for k in range(9):
                total = total + el_ref[i * 9 + k].astype(F32)
            return total
        total = lax.fori_loop(0, 7, body, total)
        out_ref[:, COLS - 128 :] = total[0] / total[1]

    def compute(ch, between):
        block, cb, group = CHUNKS[ch]
        ya, yb = (ya2, yb2) if cb == 2 else (ya1, yb1)
        ng = T // group

        def images(g, parity):
            for u in range(group):
                t = 2 * g * group + 2 * parity + u
                prepare_image(t, g * group + u, x_ref, (pe, po)[parity])

        def bands(g, parity):
            for u in range(group):
                t = 2 * g * group + 2 * parity + u
                prepare_band(t, g * group + u, (ve, vo)[parity], v0_ref)

        def where(g, parity):
            return (pe, po)[parity], (ve, vo)[parity], g * group, 2 * g * group + 2 * parity

        def filters(g, parity, y):
            p, v, slot, t = where(g, parity)
            filter_columns(slot, group, block, cb, p, h_ref, y)

        def matches(g, parity, y):
            p, v, slot, t = where(g, parity)
            match_rows(t, slot, group, block, cb, v, y, var_ref, kp_ref, sum_ref)

        if ch == 0:
            for g, parity in ((0, 0), (0, 1), (1, 0)):
                images(g, parity)
                bands(g, parity)
            for cp in cpv:
                cp.wait()
        filters(0, 0, ya)

        def body(i, carry):
            after = jnp.minimum(i + 2, ng // 2 - 1)
            filters(i, 1, yb)
            if ch == 0:
                images(i + 1, 1)
            matches(i, 0, ya)
            if ch == 0:
                bands(after, 0)
            filters(i + 1, 0, ya)
            if ch == 0:
                images(after, 0)
            matches(i, 1, yb)
            if ch == 0:
                bands(i + 1, 1)
            for turn, step in between:
                pl.when(i == turn)(step)
            return carry

        lax.fori_loop(0, ng // 2 - 1, body, 0)
        filters(ng // 2 - 1, 1, yb)
        matches(ng // 2 - 1, 0, ya)
        matches(ng // 2 - 1, 1, yb)

    compute(0, ())
    pl.semaphore_wait(barrier, 64)
    start_core(0)
    compute(1, ((0, functools.partial(start_1, 0, (0,))), (1, functools.partial(start_1, 0, (1,)))))
    start_core(1)
    compute(2, ((0, functools.partial(start_1, 1)),))
    last_core()
    last_spread()
    start_2(0)
    start_2(1)
    finish(0)
    finish(1)
    last_finish()

    for dz in range(4):
        last_copy(dz).wait_send()
    settle(el_ref, els)
    for ch in range(n - 1):
        for u in range(units(ch)):
            core_copy(ch, u).wait_send()
            settle(r1_refs[ch].at[u], s1s.at[ch, u])
            settle(r2_refs[ch].at[u], s2s.at[ch, u])


def on_device(warp_image, warp_variance, kernel_coef, tile_patch):
    basis, horizontal, vertical = tables()
    images = jnp.transpose(warp_image, (1, 0, 2)).reshape(84 * T, COLS)
    vmem = pl.BlockSpec(memory_space=pltpu.VMEM)
    smem = pl.BlockSpec(memory_space=pltpu.SMEM)
    hbm = pl.BlockSpec(memory_space=pl.ANY)
    dma = pltpu.SemaphoreType.DMA
    units = [chunk[1] for chunk in CHUNKS[:-1]]
    out = pl.pallas_call(
        kernel,
        out_shape=jax.ShapeDtypeStruct((ROWS // 4, COLS), F32),
        in_specs=[hbm, hbm, vmem, smem, vmem, hbm, vmem],
        out_specs=vmem,
        scratch_shapes=[
            pltpu.VMEM((4, 84 * T, 128), F32),
            pltpu.VMEM((T, ROWS, COLS), F32),
            pltpu.VMEM((256, NK * 128), BF16),
            pltpu.VMEM((T // 2, PROWS, 256), BF16),
            pltpu.VMEM((T // 2, PROWS, 256), BF16),
            pltpu.VMEM((T // 2, ROWS, KDIM), BF16),
            pltpu.VMEM((T // 2, ROWS, KDIM), BF16),
            pltpu.VMEM((T, KDIM), F32),
            pltpu.VMEM((2, KDIM, 256), BF16),
            pltpu.VMEM((2, KDIM, 256), BF16),
            pltpu.VMEM((4, KDIM, 128), BF16),
            pltpu.VMEM((4, KDIM, 128), BF16),
            pltpu.VMEM((T, 1, 256), F32),
            pltpu.VMEM((2, T + 1, ROWS, 256), F32),
            pltpu.VMEM((16, 128), jnp.int32),
            pltpu.SMEM((16, 128), jnp.int32),
            pltpu.VMEM((2, 64, 2, 16, 128), F32),
            *[pltpu.VMEM((u, 64, 2, 16, 128), BF16) for u in units],
            *[pltpu.VMEM((u, 64, 2, 16, 128), BF16) for u in units],
            *[pltpu.VMEM((u, 3, 16, 2, 16, 128), BF16) for u in units],
            *[pltpu.VMEM((u, 16, 2, 16, 128), BF16) for u in units],
            *[pltpu.VMEM((u, 15, 2, 16, 128), BF16) for u in units],
            pltpu.VMEM((4, 16, 2, 16, 128), BF16),
            pltpu.VMEM((4, 16, 2, 16, 128), F32),
            pltpu.VMEM((4, 16, 2, 16, 128), BF16),
            pltpu.VMEM((63, 2, 16, 128), BF16),
            dma((24,)), dma((T,)), dma, dma,
            *[dma((len(units), 2))] * 6,
            dma((4,)), dma((4,)), dma, dma,
        ],
        compiler_params=pltpu.CompilerParams(
            collective_id=0, has_side_effects=True, vmem_limit_bytes=60 * 2**20),
        name="coadd",
    )(images, warp_variance, kernel_coef, tile_patch.reshape(1, T),
      jnp.asarray(basis), jnp.asarray(horizontal), jnp.asarray(vertical))
    return out[None]


def solution(mesh):
    return jax.shard_map(
        on_device,
        mesh=mesh,
        in_specs=(
            P(("visit", "patch"), None, None),
            P(("visit", "patch"), None, None),
            P(("visit", "patch"), None),
            P(("visit", "patch"), None),
        ),
        out_specs=P("patch", "visit", None),
        check_vma=False,
    )
```

```python
import functools

import jax
import jax.numpy as jnp
import numpy as np
from jax import lax
from jax.experimental import pallas as pl
from jax.experimental.pallas import tpu as pltpu
from jax.sharding import PartitionSpec as P

KHALF = 10
TAPS = 2 * KHALF + 1
T = 24
ROWS = 64
COLS = 512
NPATCH = 32
BLK = 88
NK = 14
KDIM = 1280
CHUNKS = ((0, 2, 2), (2, 1, 4), (3, 1, 4))
PROWS = 368
PAT = (0, 88, 176, 272)
HI = lax.Precision.HIGHEST
F32 = jnp.float32
BF16 = jnp.bfloat16
MESH = pl.DeviceIdType.MESH


def tables():
    offsets = np.arange(TAPS, dtype=np.float64) - KHALF
    scaled = offsets / KHALF
    functions, place, terms = [], {}, []
    levels = ((1.0, 4), (2.5, 4), (5.0, 3))
    for s, (spread, degree) in enumerate(levels):
        profile = np.exp(-offsets * offsets / (2.0 * spread * spread))
        for i in range(degree + 1):
            place[s, i] = len(functions)
            functions.append(profile * scaled**i)
    for s, (spread, degree) in enumerate(levels):
        for i in range(degree + 1):
            for j in range(degree + 1 - i):
                terms.append((place[s, i], place[s, j]))
    g = np.array(functions)
    basis = np.zeros((len(terms), 512))
    for b, (ia, jb) in enumerate(terms):
        basis[b, : TAPS * TAPS] = np.outer(g[ia], g[jb]).reshape(-1)
    q = np.linalg.qr(g.T)[0]
    q = q.astype(jnp.bfloat16).astype(np.float64)
    mix = np.linalg.lstsq(q, g.T, rcond=None)[0]
    horizontal = np.zeros((256, NK * 128))
    for k in range(NK):
        for c in range(128):
            horizontal[c : c + TAPS, k * 128 + c] = q[:, k]
    vertical = np.zeros((len(terms), KDIM))
    for b, (ia, jb) in enumerate(terms):
        for k in range(NK):
            vertical[b, k * BLK : k * BLK + TAPS] = g[ia] * mix[k, jb]
    return basis.astype(np.float32), horizontal.astype(jnp.bfloat16), vertical.astype(np.float32)


def prepare_image(t, slot, x_ref, p_ref):
    x = jnp.concatenate([x_ref.at[j][pl.ds(t, 84, stride=T), :] for j in range(4)], axis=1)
    x = jnp.concatenate([x, jnp.zeros((BLK - 84, COLS), F32)], axis=0)
    x = jnp.concatenate([x, jnp.zeros((BLK, 128), F32)], axis=1)
    x = pltpu.roll(x, KHALF, 1)
    blocks = [x[:, 128 * j : 128 * j + 256] for j in range(4)]
    blocks.insert(3, jnp.zeros((8, 256), F32))
    blocks.append(jnp.zeros((8, 256), F32))
    p_ref[slot] = jnp.concatenate(blocks, axis=0).astype(BF16)


def prepare_band(t, slot, v_ref, v0_ref):
    row = jnp.broadcast_to(v0_ref[pl.ds(t, 1), :], (ROWS, KDIM))
    v_ref[slot] = pltpu.roll(row, 0, 1, stride=1, stride_axis=0).astype(BF16)


def filter_columns(first, group, block, cb, p_ref, h_ref, y_ref):
    rows = BLK * cb
    lhs = jnp.concatenate([p_ref[first + u, PAT[block] : PAT[block] + rows, :] for u in range(group)], axis=0)
    for m in range(NK // 2):
        r = jnp.dot(lhs, h_ref[:, 256 * m : 256 * m + 256], preferred_element_type=F32)
        for u in range(group):
            for b in range(cb):
                o = rows * u + BLK * b
                y = jnp.concatenate([r[o : o + BLK, :128], r[o : o + BLK, 128:]], axis=0)
                y_ref[u, 2 * BLK * m : 2 * BLK * m + 2 * BLK, 128 * b : 128 * b + 128] = y.astype(BF16)


def match_rows(tiles, first, group, block, cb, v_ref, y_ref, var_ref, kp_ref, sum_ref):
    cols = slice(128 * block, 128 * block + 128 * cb)
    for u in range(group):
        t = tiles + 4 * (u // 2) + u % 2
        matched = jnp.dot(v_ref[first + u], y_ref[u], preferred_element_type=F32)
        w = (1.0 / (var_ref[t, :, cols] * kp_ref[t][:, : 128 * cb])).astype(BF16).astype(F32)
        sum_ref[0, t, :, : 128 * cb] = w * matched
        sum_ref[1, t, :, : 128 * cb] = w


def place_coefs(a):
    cx = jnp.where(a == 0, 16, jnp.where(a == 1, 1, 4))
    cy = jnp.where(a == 0, 4, jnp.where(a == 1, 16, 1))
    cz = jnp.where(a == 0, 1, jnp.where(a == 1, 4, 16))
    return cx, cy, cz


def kernel(
    x_hbm, var_hbm, c_ref, tp_ref, bp_ref, h_hbm, a_ref, out_ref,
    x_ref, var_ref, h_ref, pe, po, ve, vo, v0_ref, ya2, yb2, ya1, yb1, kp_ref, sum_ref,
    iv_ref, idx_ref, own_ref, *rest,
):
    n = len(CHUNKS)
    m = n - 1
    dl_ref, ol_ref, rl_ref, el_ref = rest[5 * m : 5 * m + 4]
    sx, sv, si, sh, cs, cr, s1s, s1r, s2s, s2r, cls, clr, els, elr = rest[5 * m + 4 :]
    d_refs, rc_refs, r1_refs, s1_refs, r2_refs = (rest[i * m : i * m + m] for i in range(5))
    me_x = lax.axis_index("visit")
    me_p = lax.axis_index("patch")
    core = lax.rem(me_p, 2)
    me_y = lax.rem(me_p // 2, 4)
    me_z = me_p // 8

    def device(x, y, z, k):
        return (x, z * 8 + y * 2 + k)

    sibling = device(me_x, me_y, me_z, 1 - core)

    cpx = [
        pltpu.make_async_copy(
            x_hbm.at[pl.ds(T * 14 * (i // 4), T * 14), pl.ds(128 * (i % 4), 128)],
            x_ref.at[i % 4, pl.ds(T * 14 * (i // 4), T * 14)], sx.at[i])
        for i in range(24)
    ]
    cpv = [pltpu.make_async_copy(var_hbm.at[t], var_ref.at[t], sv.at[t]) for t in range(T)]
    cph = pltpu.make_async_copy(h_hbm, h_ref, sh)
    for cp in cpx + [cph] + cpv:
        cp.start()

    barrier = pltpu.get_barrier_semaphore()
    pl.semaphore_signal(barrier, inc=1, device_id=sibling, device_id_type=MESH)
    for d in range(1, 64):
        who = device(lax.rem(me_x + d // 4 % 4, 4), lax.rem(me_y + d % 4, 4), lax.rem(me_z + d // 16, 4), core)
        pl.semaphore_signal(barrier, inc=1, device_id=who, device_id_type=MESH)

    lane = lax.broadcasted_iota(jnp.int32, (8, 128), 1)
    one = jnp.full((8, 128), T, jnp.int32)
    two = one
    for t in range(T):
        hit = lane == tp_ref[0, t]
        two = jnp.where(hit, one, two)
        one = jnp.where(hit, t, one)
    iv_ref[0:8, :] = one
    iv_ref[8:16, :] = two
    cpi = pltpu.make_async_copy(iv_ref, idx_ref, si)
    cpi.start()

    c = c_ref[...]
    taps = jnp.dot(c, bp_ref[...], precision=HI, preferred_element_type=F32)
    kp = jnp.sum(taps * taps, axis=1, keepdims=True) / float(TAPS * TAPS) + 1e-6
    for t in range(T):
        kp_ref[t] = jnp.broadcast_to(kp[t : t + 1], (1, 256))
    v0_ref[...] = jnp.dot(c, a_ref[...], precision=HI, preferred_element_type=F32)
    for y in (ya2, yb2, ya1, yb1):
        for u in range(y.shape[0]):
            y[u, NK * BLK :, :] = jnp.zeros((KDIM - NK * BLK, y.shape[2]), BF16)
    for nd in range(2):
        sum_ref[nd, T] = jnp.zeros((ROWS, 256), F32)
    for cp in cpx:
        cp.wait()
    cph.wait()
    cpi.wait()

    def axis_of(ch, u, k):
        return lax.rem(u + k + ch * k, 3)

    def ring(b):
        here = jnp.where(b == 0, me_x, jnp.where(b == 1, me_y, me_z))
        to_v = jnp.where(b == 0, 1, 0)
        to_p = jnp.where(b == 0, 0, jnp.where(b == 1, 2, 8))
        places = [here] + [lax.rem(here + d, 4) for d in range(1, 4)]
        return [(at, (at - here) * to_v, (at - here) * to_p) for at in places]

    def units(ch):
        return CHUNKS[ch][1]

    def gather(ch, k, store):
        cbs = CHUNKS[ch][1]

        def body(i, carry):
            z, y = i // 4, lax.rem(i, 4)
            p = z * 8 + y * 2 + k
            i1, i2 = idx_ref[0, p], idx_ref[8, p]
            for nd in range(2):
                s = sum_ref[nd, i1, :, : 128 * cbs] + sum_ref[nd, i2, :, : 128 * cbs]
                for u in range(cbs):
                    cx, cy, cz = place_coefs(axis_of(ch, u, k))
                    for x in range(4):
                        store(u, cx * x + cy * y + cz * z, nd, s[16 * x : 16 * x + 16, 128 * u : 128 * u + 128])
            return carry
        lax.fori_loop(0, 16, body, 0, unroll=4)

    def core_copy(ch, u):
        return pltpu.make_async_remote_copy(
            src_ref=d_refs[ch].at[u], dst_ref=rc_refs[ch].at[u], send_sem=cs.at[ch, u], recv_sem=cr.at[ch, u],
            device_id=sibling, device_id_type=MESH)

    def settle(ref, sem):
        pltpu.make_async_copy(ref, ref, sem).wait()

    def start_core(ch):
        def put(u, place, nd, value):
            d_refs[ch][u, place, nd] = value.astype(BF16)
        gather(ch, 1 - core, put)
        for u in range(units(ch)):
            core_copy(ch, u).start()

        def keep(u, place, nd, value):
            own_ref[u, place, nd] = value
        gather(ch, core, keep)

    def start_1(ch, some=None):
        for u in some or range(units(ch)):
            core_copy(ch, u).wait_recv()
            around = ring(axis_of(ch, u, core))

            def body(i, carry):
                at = pl.ds(i * 4, 4)
                rc_refs[ch][u, at] = (rc_refs[ch][u, at].astype(F32) + own_ref[u, at]).astype(BF16)
                return carry
            lax.fori_loop(0, 16, body, 0)
            for d in (2, 1, 3):
                there, v, p = around[d]
                pltpu.make_async_remote_copy(
                    src_ref=rc_refs[ch].at[u, pl.ds(there * 16, 16)], dst_ref=r1_refs[ch].at[u, d - 1],
                    send_sem=s1s.at[ch, u], recv_sem=s1r.at[ch, u],
                    device_id=(me_x + v, me_p + p), device_id_type=MESH).start()

    def start_2(ch):
        for u in range(units(ch)):
            a = axis_of(ch, u, core)
            here = ring(a)[0][0]
            second, third = ring(lax.rem(a + 1, 3)), ring(lax.rem(a + 2, 3))
            settle(r1_refs[ch].at[u], s1r.at[ch, u])
            total = rc_refs[ch][u, pl.ds(here * 16, 16)].astype(F32)
            for d in range(3):
                total = total + r1_refs[ch][u, d].astype(F32)
            s1_refs[ch][u] = total.astype(BF16)
            for d in (10, 6, 9, 11, 14, 2, 8, 5, 7, 13, 15, 1, 3, 4, 12):
                at2, v2, p2 = second[d // 4]
                at3, v3, p3 = third[d % 4]
                pltpu.make_async_remote_copy(
                    src_ref=s1_refs[ch].at[u, at2 * 4 + at3], dst_ref=r2_refs[ch].at[u, d - 1],
                    send_sem=s2s.at[ch, u], recv_sem=s2r.at[ch, u],
                    device_id=(me_x + v2 + v3, me_p + p2 + p3), device_id_type=MESH).start()

    def finish(ch):
        for u in range(units(ch)):
            a = axis_of(ch, u, core)
            here = ring(lax.rem(a + 1, 3))[0][0] * 4 + ring(lax.rem(a + 2, 3))[0][0]
            settle(r2_refs[ch].at[u], s2r.at[ch, u])
            total = s1_refs[ch][u, here].astype(F32)
            for d in range(15):
                total = total + r2_refs[ch][u, d].astype(F32)
            at = 128 * (CHUNKS[ch][0] + u)
            out_ref[:, at : at + 128] = total[0] / total[1]

    def last_gather(dz, k, store):
        z = lax.rem(me_z + dz, 4)

        def body(y, carry):
            p = z * 8 + y * 2 + k
            i1, i2 = idx_ref[0, p], idx_ref[8, p]
            for nd in range(2):
                s = sum_ref[nd, i1, :, :128] + sum_ref[nd, i2, :, :128]
                for x in range(4):
                    store(dz, x * 4 + y, nd, s[16 * x : 16 * x + 16])
            return carry
        lax.fori_loop(0, 4, body, 0, unroll=4)

    def last_copy(dz):
        return pltpu.make_async_remote_copy(
            src_ref=dl_ref.at[dz], dst_ref=rl_ref.at[dz], send_sem=cls.at[dz], recv_sem=clr.at[dz],
            device_id=sibling, device_id_type=MESH)

    def last_core():
        def put(dz, place, nd, value):
            dl_ref[dz, place, nd] = value.astype(BF16)

        def keep(dz, place, nd, value):
            ol_ref[dz, place, nd] = value
        for dz in (2, 1, 3, 0):
            last_gather(dz, 1 - core, put)
            last_copy(dz).start()
        for dz in (2, 1, 3, 0):
            last_gather(dz, core, keep)

    def last_spread():
        for dz in (2, 1, 3, 0):
            last_copy(dz).wait_recv()
            rl_ref[dz] = (rl_ref[dz].astype(F32) + ol_ref[dz]).astype(BF16)
            z = lax.rem(me_z + dz, 4)
            for dx in (2, 1, 3, 0):
                x = lax.rem(me_x + dx, 4)
                for dy in (2, 1, 3, 0):
                    y = lax.rem(me_y + dy, 4)
                    slot = dz * 16 + dx * 4 + dy - 1
                    if slot >= 0:
                        pltpu.make_async_remote_copy(
                            src_ref=rl_ref.at[dz, x * 4 + y], dst_ref=el_ref.at[slot], send_sem=els, recv_sem=elr,
                            device_id=device(x, y, z, core), device_id_type=MESH).start()

    def last_finish():
        settle(el_ref, elr)
        total = rl_ref[0, me_x * 4 + me_y].astype(F32)

        def body(i, total):
            for k in range(9):
                total = total + el_ref[i * 9 + k].astype(F32)
            return total
        total = lax.fori_loop(0, 7, body, total)
        out_ref[:, COLS - 128 :] = total[0] / total[1]

    def compute(ch, between):
        block, cb, group = CHUNKS[ch]
        ya, yb = (ya2, yb2) if cb == 2 else (ya1, yb1)
        ng = T // group

        def images(g, parity):
            for u in range(group):
                t = 2 * g * group + 2 * parity + u
                prepare_image(t, g * group + u, x_ref, (pe, po)[parity])

        def bands(g, parity):
            for u in range(group):
                t = 2 * g * group + 2 * parity + u
                prepare_band(t, g * group + u, (ve, vo)[parity], v0_ref)

        def where(g, parity):
            return (pe, po)[parity], (ve, vo)[parity], g * group, 2 * g * group + 2 * parity

        def filters(g, parity, y):
            p, v, slot, t = where(g, parity)
            filter_columns(slot, group, block, cb, p, h_ref, y)

        def matches(g, parity, y):
            p, v, slot, t = where(g, parity)
            match_rows(t, slot, group, block, cb, v, y, var_ref, kp_ref, sum_ref)

        if ch == 0:
            for g, parity in ((0, 0), (0, 1), (1, 0)):
                images(g, parity)
                bands(g, parity)
            for cp in cpv:
                cp.wait()
        filters(0, 0, ya)

        def body(i, carry):
            after = jnp.minimum(i + 2, ng // 2 - 1)
            filters(i, 1, yb)
            if ch == 0:
                images(i + 1, 1)
            matches(i, 0, ya)
            for turn, step in between:
                if turn < 0:
                    pl.when(i == 0)(step)
            if ch == 0:
                bands(after, 0)
            filters(i + 1, 0, ya)
            if ch == 0:
                images(after, 0)
            matches(i, 1, yb)
            if ch == 0:
                bands(i + 1, 1)
            for turn, step in between:
                if turn >= 0:
                    pl.when(i == turn)(step)
            return carry

        lax.fori_loop(0, ng // 2 - 1, body, 0)
        filters(ng // 2 - 1, 1, yb)
        matches(ng // 2 - 1, 0, ya)
        matches(ng // 2 - 1, 1, yb)

    compute(0, ())
    pl.semaphore_wait(barrier, 64)
    start_core(0)
    compute(1, ((0, functools.partial(start_1, 0, (0,))), (1, functools.partial(start_1, 0, (1,)))))
    start_core(1)
    compute(2, ((-1, functools.partial(start_1, 1)),))
    last_core()
    last_spread()
    start_2(0)
    start_2(1)
    finish(0)
    finish(1)
    last_finish()

    for dz in range(4):
        last_copy(dz).wait_send()
    settle(el_ref, els)
    for ch in range(n - 1):
        for u in range(units(ch)):
            core_copy(ch, u).wait_send()
            settle(r1_refs[ch].at[u], s1s.at[ch, u])
            settle(r2_refs[ch].at[u], s2s.at[ch, u])


def on_device(warp_image, warp_variance, kernel_coef, tile_patch):
    basis, horizontal, vertical = tables()
    images = jnp.transpose(warp_image, (1, 0, 2)).reshape(84 * T, COLS)
    vmem = pl.BlockSpec(memory_space=pltpu.VMEM)
    smem = pl.BlockSpec(memory_space=pltpu.SMEM)
    hbm = pl.BlockSpec(memory_space=pl.ANY)
    dma = pltpu.SemaphoreType.DMA
    units = [chunk[1] for chunk in CHUNKS[:-1]]
    out = pl.pallas_call(
        kernel,
        out_shape=jax.ShapeDtypeStruct((ROWS // 4, COLS), F32),
        in_specs=[hbm, hbm, vmem, smem, vmem, hbm, vmem],
        out_specs=vmem,
        scratch_shapes=[
            pltpu.VMEM((4, 84 * T, 128), F32),
            pltpu.VMEM((T, ROWS, COLS), F32),
            pltpu.VMEM((256, NK * 128), BF16),
            pltpu.VMEM((T // 2, PROWS, 256), BF16),
            pltpu.VMEM((T // 2, PROWS, 256), BF16),
            pltpu.VMEM((T // 2, ROWS, KDIM), BF16),
            pltpu.VMEM((T // 2, ROWS, KDIM), BF16),
            pltpu.VMEM((T, KDIM), F32),
            pltpu.VMEM((2, KDIM, 256), BF16),
            pltpu.VMEM((2, KDIM, 256), BF16),
            pltpu.VMEM((4, KDIM, 128), BF16),
            pltpu.VMEM((4, KDIM, 128), BF16),
            pltpu.VMEM((T, 1, 256), F32),
            pltpu.VMEM((2, T + 1, ROWS, 256), F32),
            pltpu.VMEM((16, 128), jnp.int32),
            pltpu.SMEM((16, 128), jnp.int32),
            pltpu.VMEM((2, 64, 2, 16, 128), F32),
            *[pltpu.VMEM((u, 64, 2, 16, 128), BF16) for u in units],
            *[pltpu.VMEM((u, 64, 2, 16, 128), BF16) for u in units],
            *[pltpu.VMEM((u, 3, 16, 2, 16, 128), BF16) for u in units],
            *[pltpu.VMEM((u, 16, 2, 16, 128), BF16) for u in units],
            *[pltpu.VMEM((u, 15, 2, 16, 128), BF16) for u in units],
            pltpu.VMEM((4, 16, 2, 16, 128), BF16),
            pltpu.VMEM((4, 16, 2, 16, 128), F32),
            pltpu.VMEM((4, 16, 2, 16, 128), BF16),
            pltpu.VMEM((63, 2, 16, 128), BF16),
            dma((24,)), dma((T,)), dma, dma,
            *[dma((len(units), 2))] * 6,
            dma((4,)), dma((4,)), dma, dma,
        ],
        compiler_params=pltpu.CompilerParams(
            collective_id=0, has_side_effects=True, vmem_limit_bytes=60 * 2**20),
        name="coadd",
    )(images, warp_variance, kernel_coef, tile_patch.reshape(1, T),
      jnp.asarray(basis), jnp.asarray(horizontal), jnp.asarray(vertical))
    return out[None]


def solution(mesh):
    return jax.shard_map(
        on_device,
        mesh=mesh,
        in_specs=(
            P(("visit", "patch"), None, None),
            P(("visit", "patch"), None, None),
            P(("visit", "patch"), None),
            P(("visit", "patch"), None),
        ),
        out_specs=P("patch", "visit", None),
        check_vma=False,
    )
```
